512 devices in a mesh: rows: 8 (over z), ctx: 64 (over x, y, core).
Axes of the slice: x: 4, y: 8, z: 8, core: 2. Of those that a mesh axis runs over, the one named last changes fastest.
Arguments:
- nope_query: bfloat16 [8, 2, 128, 128], P('rows', None, 'ctx'), may hold values from -6 to 6
- rope_query: bfloat16 [8, 2, 128, 64], P('rows', None, 'ctx'), may hold values from -6 to 6
- key_lift: bfloat16 [128, 128, 512], P('ctx'), may hold values from -2 to 2
- value_lift: bfloat16 [128, 512, 128], P('ctx'), may hold values from -0.25 to 0.25
- out_weight: bfloat16 [16384, 7168], P('ctx', 'rows'), may hold values from -0.125 to 0.125
- latent_cache: bfloat16 [8, 65536, 576], P('rows', 'ctx'), may hold values from -100 to 100
- lengths: int32 [8], P('rows'), may hold values from 2 to 65536, as said below
Outputs:
- layer_out: float32 [8, 2, 7168], P(None, None, ('rows', 'ctx'))
The draws below stay inside these ranges and needn't reach their ends.
Inputs may be any that keep to these rules, and one draw needn't show every extreme that they name: `lengths`: in every draw one sequence has exactly 65536 cached positions.
All inputs are finite; a program needn't handle non-finite values.
Results may differ from the reference program's by a relative error of at most 0.0099.
Values may be sent and summed in bfloat16 or wider, within the bound.
A program may use at most 128 MiB of HBM per device.

```python
import jax
import jax.numpy as jnp
from jax import lax

H = 128
DN = 128
DR = 64
LAT = 512
DV = 128
D = 7168
QLEN = 2
SEQS = 8
CTXLEN = 65536


def rope_common(key, exponent):
    normal_draw = jnp.clip(jax.random.normal(key, (SEQS, QLEN, H, DR), jnp.float32), -6.0, 6.0)
    return jnp.sign(normal_draw) * jnp.abs(normal_draw) ** exponent


def draw_rope_query(key, part):
    values = rope_common(key, 1.0)
    return values.astype(jnp.bfloat16)


def draw_latent_cache(key, part):
    key = jax.random.fold_in(key, 7)
    subkeys = jax.random.split(key, 2)
    values = jnp.clip(jax.random.normal(subkeys[1], (SEQS, CTXLEN, LAT + DR), jnp.float32), -6.0, 6.0)
    return values.astype(jnp.bfloat16)


def draw_lengths(key, part):
    key = jax.random.fold_in(key, 11)
    subkeys = jax.random.split(key, 3)
    upper = jax.random.randint(subkeys[0], (SEQS,), QLEN + 1, CTXLEN + 1)
    spans = jax.random.randint(subkeys[1], (SEQS,), 0, 1 << 30) % (upper - QLEN)
    values = QLEN + spans
    longest = jax.random.randint(subkeys[2], (), 0, SEQS)
    values = values.at[longest].set(CTXLEN)
    return values.astype(jnp.int32)


def strengthened(entries, own_key, source, target, parts, factor):
    def block_of(dim):
        return (jnp.arange(entries.shape[dim]) // (entries.shape[dim] // parts)).reshape((-1,) + (1,) * (entries.ndim - 1 - dim))

    near = jax.random.permutation(own_key, parts)[block_of(target)]
    far = (block_of(target) + parts // 2) % parts
    return jnp.where((block_of(source) == near) | (block_of(source) == far), factor * entries, entries)


def levels(rng, extent, cuts, least, largest):
    factor_of = 1.0
    for axis_at, shards_of in cuts:
        heights = jax.random.uniform(jax.random.fold_in(jax.random.fold_in(rng, 6), axis_at), (shards_of,), jnp.float32, least / len(cuts), largest / len(cuts))
        factor_of = factor_of * jnp.repeat(jnp.exp(heights), extent[axis_at] // shards_of).reshape((-1,) + (1,) * (len(extent) - 1 - axis_at))
    return factor_of


def normal_values(rng, dims, scale, limit, pieces=(), kind=jnp.bfloat16):
    values = jax.random.normal(rng, dims, jnp.float32) * scale
    if len(pieces) > 0:
        values = levels(rng, dims, pieces, -0.22, 0.18) * values
    return jnp.clip(values, min=-limit, max=limit).astype(kind)


def heavy_noise(key, dims, deviation, most, cuts, heavy, kind=jnp.bfloat16):
    array = deviation * jax.random.normal(key, dims, jnp.float32)
    if cuts:
        array = array * levels(key, dims, cuts, -0.22, 0.18)
    return jnp.clip(strengthened(array, jax.random.fold_in(key, 3), *heavy), -most, most).astype(kind)


def setup_inputs(seed: int = 0) -> dict:
    arg_keys = jax.random.split(jax.random.key(seed), 8)
    return {
        "nope_query": normal_values(arg_keys[0], (SEQS, QLEN, H, DN), 1.0, 6.0, ((0, 8), (2, 64))),
        "rope_query": draw_rope_query(jax.random.fold_in(arg_keys[7], 71), 0),
        "key_lift": normal_values(arg_keys[2], (H, DN, LAT), 0.15, 2.0, ((0, 64),)),
        "value_lift": normal_values(arg_keys[3], (H, LAT, DV), LAT ** -0.5, 0.25, ((0, 64),)),
        "out_weight": heavy_noise(arg_keys[4], (H * DV, D), (H * DV) ** -0.5, 0.125, ((0, 64), (1, 8)), (0, 1, 64, 4.0)),
        "latent_cache": draw_latent_cache(jax.random.fold_in(arg_keys[7], 71), 0),
        "lengths": draw_lengths(jax.random.fold_in(arg_keys[7], 71), 0),
    }


def attend(query, cache_rows, length):
    width = LAT + DR
    query_rows = query.reshape(QLEN * H, width)
    score_scale = (DN + DR) ** -0.5
    block_count = CTXLEN // 512
    blocks = cache_rows.reshape(block_count, 512, width)
    visible_end = length - QLEN + 1 + jnp.arange(QLEN * H, dtype=jnp.int32) // H

    def block_scores(block_index, key_block):
        scores = jnp.dot(query_rows, key_block.T, preferred_element_type=jnp.float32) * score_scale
        positions = block_index * 512 + jnp.arange(512, dtype=jnp.int32)
        visible = positions[None, :] < visible_end[:, None]
        return scores, visible

    def first_pass(running_max, item):
        block_index, key_block = item
        scores, visible = block_scores(block_index, key_block)
        highest = jnp.max(jnp.where(visible, scores, -1e30), axis=1)
        return jnp.maximum(running_max, highest), None

    indices = jnp.arange(block_count, dtype=jnp.int32)
    start_max = jnp.full((QLEN * H,), -1e30, jnp.float32)
    top = lax.scan(first_pass, start_max, (indices, blocks))[0]

    def second_pass(carry, item):
        denominator, weighted = carry
        block_index, key_block = item
        scores, visible = block_scores(block_index, key_block)
        expo = jnp.where(visible, jnp.exp(scores - top[:, None]), 0.0)
        denominator = denominator + jnp.sum(expo, axis=1)
        weighted = weighted + jnp.dot(expo.astype(jnp.bfloat16), key_block[:, :LAT], preferred_element_type=jnp.float32)
        return (denominator, weighted), None

    start = (jnp.zeros((QLEN * H,), jnp.float32), jnp.zeros((QLEN * H, LAT), jnp.float32))
    denominator, weighted = lax.scan(second_pass, start, (indices, blocks))[0]
    return (weighted / denominator[:, None]).astype(jnp.bfloat16).reshape(QLEN, H, LAT)


def reference(nope_query, rope_query, key_lift, value_lift, out_weight, latent_cache, lengths):
    latent_query = jnp.einsum("sqhn,hnl->sqhl", nope_query.astype(jnp.float32), key_lift.astype(jnp.float32)).astype(jnp.bfloat16)
    query = jnp.concatenate([latent_query, rope_query], axis=-1)
    latent_out = lax.map(lambda packed: attend(packed[0], packed[1], packed[2]), (query, latent_cache, lengths))
    head_out = jnp.einsum("sqhl,hlv->sqhv", latent_out.astype(jnp.float32), value_lift.astype(jnp.float32)).astype(jnp.bfloat16)
    flattened = head_out.reshape(SEQS * QLEN, H * DV)
    layer_out = jnp.dot(flattened, out_weight, preferred_element_type=jnp.float32)
    return layer_out.reshape(SEQS, QLEN, D)
```

```python
import functools

import jax
import jax.numpy as jnp
from jax import lax
from jax.experimental import pallas as pl
from jax.experimental.pallas import tpu as pltpu
from jax.sharding import PartitionSpec as P

DN = 128
DR = 64
LAT = 512
DV = 128
X, Y, Z = 4, 8, 8
G = 2 * X
COLS = 14
LOG2E = 1.4426950408889634
LOWEST = -1e30

MESH = pl.DeviceIdType.MESH
F32 = jnp.float32
BF16 = jnp.bfloat16

AWAY = [(dx, dc) for dx in range(X) for dc in range(2)]
ROWS = 4 * Y
ROWS_BITS = ROWS.bit_length() - 1


def iota(shape, axis):
    return lax.broadcasted_iota(jnp.int32, shape, axis)


def dot(a, b):
    return jnp.dot(a, b, preferred_element_type=F32)


def farthest_first(n):
    return sorted(range(1, n), key=lambda d: -min(d, n - d))


def one_where(condition):
    return jnp.where(condition, 1.0, 0.0).astype(BF16)


def split_three(value):
    high = value.astype(BF16)
    rest = value - high.astype(F32)
    middle = rest.astype(BF16)
    low = (rest - middle.astype(F32)).astype(BF16)
    return high, middle, low


def stat_tile(value, rows):
    high, middle, low = split_three(jnp.broadcast_to(value, (rows, 128)))
    lane = iota((rows, 128), 1)
    tile = jnp.where(
        lane == 0,
        high.astype(F32),
        jnp.where(lane == 1, middle.astype(F32), jnp.where(lane == 2, low.astype(F32), 0.0)),
    )
    return tile.astype(BF16)


def read_stat(tile):
    return jnp.sum(tile.astype(F32), axis=1, keepdims=True)


def combine(parts, stats):
    top = functools.reduce(jnp.maximum, stats)
    factors = [jnp.exp2(stat - top) for stat in stats]
    weight = functools.reduce(jnp.add, factors)
    total = functools.reduce(jnp.add, [f * p for f, p in zip(factors, parts)])
    return total / weight, top + jnp.log2(weight)


def kernel(
    lengths,
    nope_hbm,
    rope_hbm,
    key_lift_hbm,
    value_lift_hbm,
    weight_hbm,
    cache_hbm,
    out,
    nope,
    rope,
    key_lift,
    value_lift,
    weight,
    cache,
    placed,
    near_q,
    all_q,
    part_out,
    part_in,
    own_out,
    own_in,
    heads,
    sums_out,
    sums_in,
    last_out,
    last_in,
    local_sem,
    send_sem,
    recv_sem,
):
    row = lax.axis_index("rows")
    ctx = lax.axis_index("ctx")
    core = ctx & 1
    y = (ctx >> 1) & (Y - 1)
    x = ctx >> Y.bit_length()

    def along_y(d):
        return (row, (x * Y + ((y + d) & (Y - 1))) * 2 + core)

    def in_group(dx, dc):
        return (row, (((x + dx) & (X - 1)) * Y + y) * 2 + ((core + dc) & 1))

    def along_z(d):
        return ((row + d) & (Z - 1), ctx)

    loads = [
        pltpu.make_async_copy(key_lift_hbm, key_lift, local_sem.at[0]),
        pltpu.make_async_copy(cache_hbm, cache.at[0, pl.ds(0, LAT + DR)], local_sem.at[1]),
        pltpu.make_async_copy(weight_hbm, weight, local_sem.at[2]),
        pltpu.make_async_copy(value_lift_hbm, value_lift, local_sem.at[3]),
        pltpu.make_async_copy(nope_hbm, nope, local_sem.at[4]),
        pltpu.make_async_copy(rope_hbm, rope, local_sem.at[5]),
    ]
    for at in (0, 4, 5):
        loads[at].start()

    barrier = pltpu.get_barrier_semaphore()
    partners = (
        [in_group(*away) for away in AWAY[1:]]
        + [along_y(d) for d in range(1, Y)]
        + [along_z(d) for d in range(1, Z)]
    )
    for partner in partners:
        pl.semaphore_signal(barrier, inc=1, device_id=partner, device_id_type=MESH)
    for at in (1, 2, 3):
        loads[at].start()

    def send(stage, slot, source, target, device):
        copy = pltpu.make_async_remote_copy(
            src_ref=source,
            dst_ref=target,
            send_sem=send_sem.at[stage, slot],
            recv_sem=recv_sem.at[stage, slot],
            device_id=device,
            device_id_type=MESH,
        )
        copy.start()
        return copy

    row16 = iota((16, 128), 0)
    even = (row16 & 1) == 0
    for at in (4, 5, 0):
        loads[at].wait()
    nope_rows = nope[0].astype(F32)
    rope_rows = rope[0].astype(F32)
    latent = jnp.zeros((16, 128), F32)
    rotary = jnp.zeros((16, DR), F32)
    for h in range(2):
        left = jnp.where(
            even,
            jnp.broadcast_to(nope_rows[0, h : h + 1, :], (16, DN)),
            jnp.broadcast_to(nope_rows[1, h : h + 1, :], (16, DN)),
        ).astype(BF16)
        lifted = dot(left, key_lift[h])
        for c in range(4):
            latent = jnp.where(
                (row16 >> 1) == 2 * c + h, lifted[:, 128 * c : 128 * (c + 1)], latent
            )
        for j in range(2):
            rotary = jnp.where(
                row16[:, :DR] == 2 * h + j,
                jnp.broadcast_to(rope_rows[j, h : h + 1, :], (16, DR)),
                rotary,
            )
    near_q[0, 0:16, :] = latent.astype(BF16)
    near_q[0, 16:32, :] = jnp.concatenate([rotary, jnp.zeros((16, 128 - DR), F32)], axis=1).astype(BF16)
    for part in range(2):
        cache[part, LAT + DR :, :] = jnp.zeros((128 - DR, cache.shape[2]), BF16)

    pl.semaphore_wait(barrier, len(partners))

    sent = [send(0, d, near_q.at[0], near_q.at[d], along_y(d)) for d in farthest_first(Y)]
    shared = send(0, 0, cache_hbm, cache.at[1, pl.ds(0, LAT + DR)], in_group(0, 1))

    r = iota((5 * ROWS, Y * 32), 0)
    k = iota((5 * ROWS, Y * 32), 1)
    i = r & (ROWS - 1)
    spread = one_where(k == (i >> 2) * 32 + (r >> ROWS_BITS) * 4 + (i & 3))
    r = iota((Y * 32, 5 * ROWS), 0)
    k = iota((Y * 32, 5 * ROWS), 1)
    place = r & 31
    gather = one_where(k == jnp.minimum(place >> 2, 4) * ROWS + (r >> 5) * 4 + (place & 3))
    for copy in sent:
        copy.wait_recv()
    rows = dot(spread, near_q[...].reshape(Y * 32, 128))
    for c in range(5):
        all_q[0, :, 128 * c : 128 * (c + 1)] = rows[ROWS * c : ROWS * (c + 1)].astype(BF16)

    last = sent
    sent = {dx: send(1, dx, all_q.at[0], all_q.at[dx], in_group(dx, 0)) for dx in farthest_first(X)}
    for copy in last:
        copy.wait_send()

    loads[2].wait()
    span = Y * 2 * COLS
    for ax in range(X):
        low = ax * span // 128 * 128
        high = min(-(-(ax + 1) * span // 128) * 128, X * span)
        n = iota((high - low, 256), 0) + low
        lane = iota((1, 256), 1)
        to_core, to_y, column = lane >> 7, (y + ((lane & 127) >> 4)) & (Y - 1), lane & 15
        source = ((ax * Y + to_y) * 2 + to_core) * COLS + column
        source = jnp.where(column < COLS, source, -1)
        choose = one_where(n == source)
        placed[:, 256 * ax : 256 * (ax + 1)] = dot(weight[:, low:high], choose).astype(BF16)

    loads[1].wait()
    span = cache.shape[2]
    count = ROWS * X
    limit = lengths[0] - 1 + (iota((count, 1), 0) & 1)
    scale = LOG2E * (DN + DR) ** -0.5
    for copy in sent.values():
        copy.wait_recv()
    query = all_q[...].reshape(count, LAT + 128)
    scores, seen = [], []
    for part in range(2):
        if part:
            shared.wait_recv()
        owner = ctx if part == 0 else ctx + 1 - 2 * core
        visible = iota((1, span), 1) + owner * span < limit
        scores.append(jnp.where(visible, dot(query, cache[part]) * scale, LOWEST))
        seen.append(visible)
    top = jnp.max(jnp.maximum(scores[0], scores[1]), axis=1, keepdims=True)
    expos = [jnp.where(v, jnp.exp2(score - top), 0.0) for v, score in zip(seen, scores)]
    denominator = jnp.maximum(jnp.sum(expos[0] + expos[1], axis=1, keepdims=True), 1e-30)
    weighted = [
        lax.dot_general(
            expo.astype(BF16), cache[part, 0:LAT, :], (((1,), (1,)), ((), ())), preferred_element_type=F32
        )
        for part, expo in enumerate(expos)
    ]
    result = ((weighted[0] + weighted[1]) / denominator).astype(BF16)
    stats = stat_tile(top + jnp.log2(denominator), count)
    part_out[:, :, 0:LAT] = result.reshape(X, ROWS, LAT)
    part_out[:, :, LAT:] = stats.reshape(X, ROWS, 128)
    back = [
        send(2, dx, part_out.at[dx], part_in.at[dx], in_group(X - dx, 0)) for dx in farthest_first(X)
    ]
    for copy in sent.values():
        copy.wait_send()
    shared.wait_send()

    loads[3].wait()
    for copy in back:
        copy.wait_recv()
    held = [part_out[0]] + [part_in[dx] for dx in range(1, X)]
    total, stat = combine(
        [part[:, 0:LAT].astype(F32) for part in held], [read_stat(part[:, LAT:]) for part in held]
    )
    total = total.astype(BF16)
    stacked = jnp.concatenate(
        [total[:, 128 * c : 128 * (c + 1)] for c in range(4)] + [stat_tile(stat, ROWS)], axis=0
    )
    own_out[...] = dot(gather, stacked).astype(BF16).reshape(Y, 32, 128)

    sent = [send(3, d, own_out.at[d], own_in.at[d], along_y(Y - d)) for d in farthest_first(Y)]
    for copy in back:
        copy.wait_send()
    r = iota((128, 16), 0)
    k = iota((128, 16), 1)
    to_row = r & 15
    block = r >> 4
    source = (block & 3) * 4 + (block >> 2) * 2 + (to_row & 1)
    pick = one_where(k == source)
    for copy in sent:
        copy.wait_recv()
    held = [own_out[0]] + [own_in[d] for d in range(1, Y)]
    latent_out, _ = combine(
        [part[0:16].astype(F32) for part in held], [read_stat(part[16:32]) for part in held]
    )
    picked = dot(pick, latent_out.astype(BF16)).astype(BF16)
    for h in range(2):
        wide = jnp.concatenate([picked[64 * h + 16 * c : 64 * h + 16 * (c + 1)] for c in range(4)], axis=1)
        heads[0, :, DV * h : DV * (h + 1)] = dot(wide, value_lift[h])[0:2].astype(BF16).astype(F32)

    last = sent
    sent = [send(4, d, heads.at[0], heads.at[d], along_z(d)) for d in farthest_first(Z)]
    for copy in last:
        copy.wait_send()
    for copy in sent:
        copy.wait_recv()
    every = jnp.concatenate([heads[d] for d in range(Z)], axis=0).astype(BF16)
    product = dot(every, placed[...])
    for g in range(G):
        sums_out[g] = product[:, 128 * g : 128 * (g + 1)]

    last = sent
    sent = []
    for g in sorted(range(1, G), key=lambda g: -min(AWAY[g][0], X - AWAY[g][0])):
        dx, dc = AWAY[g]
        chunk = ((x + dx) & (X - 1)) * 2 + ((core + dc) & 1)
        sent.append(send(5, g, sums_out.at[chunk], sums_in.at[g], in_group(dx, dc)))
    for copy in last:
        copy.wait_send()
    for copy in sent:
        copy.wait_recv()
    total = functools.reduce(jnp.add, [sums_in[g] for g in range(1, G)]) + sums_out[x * 2 + core]

    came_from = ((iota((8, 128), 1) >> 4) - iota((8, 128), 0)) & 7
    for half in range(2):
        turned = pltpu.roll(total[8 * half : 8 * half + 8], 0, 1, stride=16, stride_axis=0)
        for d in range(Y):
            line = jnp.sum(jnp.where(came_from == d, turned, 0.0), axis=0, keepdims=True)
            last_out[d, half : half + 1, :] = pltpu.roll(line, (128 - 16 * d) & 127, 1)
    last = sent
    sent = [send(6, d, last_out.at[d], last_in.at[d], along_y(d)) for d in farthest_first(Y)]
    for copy in last:
        copy.wait_send()
    for copy in sent:
        copy.wait_recv()
    total = functools.reduce(jnp.add, [last_in[d] for d in range(1, Y)]) + last_out[0]
    for half in range(2):
        wide = jnp.broadcast_to(total[half : half + 1], (8, 128))
        wide = pltpu.roll(wide, 16, 1, stride=16, stride_axis=0)
        for at in range(8):
            sequence = (row - (4 * half + at // 2)) & (Z - 1)
            out[sequence, at % 2 : at % 2 + 1, :] = wide[7 - at : 8 - at, 0:COLS]
    for copy in sent:
        copy.wait_send()


def on_device(nope_query, rope_query, key_lift, value_lift, out_weight, latent_cache, lengths):
    cache = latent_cache[0].T
    in_hbm = (nope_query, rope_query, key_lift, value_lift, out_weight, cache)
    span = cache.shape[1]
    most = max(G, Y)
    vmem = pl.BlockSpec(memory_space=pltpu.VMEM)
    hbm = pl.BlockSpec(memory_space=pltpu.HBM)
    return pl.pallas_call(
        kernel,
        out_shape=jax.ShapeDtypeStruct((Z, 2, COLS), F32),
        in_specs=[pl.BlockSpec(memory_space=pltpu.SMEM)] + [hbm] * 6,
        out_specs=vmem,
        scratch_shapes=[
            pltpu.VMEM(nope_query.shape, BF16),
            pltpu.VMEM(rope_query.shape, BF16),
            pltpu.VMEM(key_lift.shape, BF16),
            pltpu.VMEM(value_lift.shape, BF16),
            pltpu.VMEM(out_weight.shape, BF16),
            pltpu.VMEM((2, LAT + 128, span), BF16),
            pltpu.VMEM((2 * DV, 128 * G), BF16),
            pltpu.VMEM((Y, 32, 128), BF16),
            pltpu.VMEM((X, ROWS, LAT + 128), BF16),
            pltpu.VMEM((X, ROWS, LAT + 128), BF16),
            pltpu.VMEM((X, ROWS, LAT + 128), BF16),
            pltpu.VMEM((Y, 32, 128), BF16),
            pltpu.VMEM((Y, 32, 128), BF16),
            pltpu.VMEM((Z, 2, 2 * DV), F32),
            pltpu.VMEM((G, 16, 128), F32),
            pltpu.VMEM((G, 16, 128), F32),
            pltpu.VMEM((Y, 2, 128), F32),
            pltpu.VMEM((Y, 2, 128), F32),
            pltpu.SemaphoreType.DMA((6,)),
            pltpu.SemaphoreType.DMA((7, most)),
            pltpu.SemaphoreType.DMA((7, most)),
        ],
        compiler_params=pltpu.CompilerParams(
            collective_id=0, has_side_effects=True, vmem_limit_bytes=32 << 20
        ),
        cost_estimate=pl.CostEstimate(flops=600_000_000, bytes_accessed=2_500_000, transcendentals=300_000),
    )(lengths, *(pltpu.with_memory_space_constraint(a, pltpu.HBM) for a in in_hbm))


def solution(mesh):
    in_specs = (
        P("rows", None, "ctx", None),
        P("rows", None, "ctx", None),
        P("ctx", None, None),
        P("ctx", None, None),
        P("ctx", "rows"),
        P("rows", "ctx", None),
        P("rows"),
    )
    out_specs = P(None, None, ("rows", "ctx"))
    return jax.shard_map(
        on_device, mesh=mesh, in_specs=in_specs, out_specs=out_specs, check_vma=False
    )
```

```python
import functools

import jax
import jax.numpy as jnp
from jax import lax
from jax.experimental import pallas as pl
from jax.experimental.pallas import tpu as pltpu
from jax.sharding import PartitionSpec as P

DN = 128
DR = 64
LAT = 512
DV = 128
X, Y, Z = 4, 8, 8
G = 2 * X
COLS = 14
LOG2E = 1.4426950408889634
LOWEST = -1e30

MESH = pl.DeviceIdType.MESH
F32 = jnp.float32
BF16 = jnp.bfloat16

AWAY = [(dx, dc) for dx in range(X) for dc in range(2)]
ROWS = 4 * Y
ROWS_BITS = ROWS.bit_length() - 1


def iota(shape, axis):
    return lax.broadcasted_iota(jnp.int32, shape, axis)


def dot(a, b):
    return jnp.dot(a, b, preferred_element_type=F32)


def farthest_first(n):
    return sorted(range(1, n), key=lambda d: -min(d, n - d))


def one_where(condition):
    return jnp.where(condition, 1.0, 0.0).astype(BF16)


def split_three(value):
    high = value.astype(BF16)
    rest = value - high.astype(F32)
    middle = rest.astype(BF16)
    low = (rest - middle.astype(F32)).astype(BF16)
    return high, middle, low


def stat_tile(value, rows):
    high, middle, low = split_three(jnp.broadcast_to(value, (rows, 128)))
    lane = iota((rows, 128), 1)
    tile = jnp.where(
        lane == 0,
        high.astype(F32),
        jnp.where(lane == 1, middle.astype(F32), jnp.where(lane == 2, low.astype(F32), 0.0)),
    )
    return tile.astype(BF16)


def read_stat(tile):
    return jnp.sum(tile.astype(F32), axis=1, keepdims=True)


def blocks_transposed(tile):
    row, block = iota((8, 128), 0), iota((8, 128), 1) >> 4
    for step in (1, 2, 4):
        above = pltpu.roll(pltpu.roll(tile, 8 - step, 0), 16 * step, 1)
        below = pltpu.roll(pltpu.roll(tile, step, 0), 128 - 16 * step, 1)
        stays = (row & step) == (block & step)
        tile = jnp.where(stays, tile, jnp.where((row & step) == 0, above, below))
    return tile


def combine(parts, stats):
    top = functools.reduce(jnp.maximum, stats)
    factors = [jnp.exp2(stat - top) for stat in stats]
    weight = functools.reduce(jnp.add, factors)
    total = functools.reduce(jnp.add, [f * p for f, p in zip(factors, parts)])
    return total / weight, top + jnp.log2(weight)


def kernel(
    lengths,
    nope_hbm,
    rope_hbm,
    key_lift_hbm,
    value_lift_hbm,
    weight_hbm,
    cache_hbm,
    out,
    nope,
    rope,
    key_lift,
    value_lift,
    weight,
    cache,
    placed,
    near_q,
    all_q,
    part_out,
    part_in,
    own_out,
    own_in,
    heads,
    sums_out,
    sums_in,
    local_sem,
    send_sem,
    recv_sem,
):
    row = lax.axis_index("rows")
    ctx = lax.axis_index("ctx")
    core = ctx & 1
    y = (ctx >> 1) & (Y - 1)
    x = ctx >> Y.bit_length()

    def along_y(d):
        return (row, (x * Y + ((y + d) & (Y - 1))) * 2 + core)

    def in_group(dx, dc):
        return (row, (((x + dx) & (X - 1)) * Y + y) * 2 + ((core + dc) & 1))

    def along_z(d):
        return ((row + d) & (Z - 1), ctx)

    loads = [
        pltpu.make_async_copy(key_lift_hbm, key_lift, local_sem.at[0]),
        pltpu.make_async_copy(cache_hbm, cache.at[0, pl.ds(0, LAT + DR)], local_sem.at[1]),
        pltpu.make_async_copy(weight_hbm, weight, local_sem.at[2]),
        pltpu.make_async_copy(value_lift_hbm, value_lift, local_sem.at[3]),
        pltpu.make_async_copy(nope_hbm, nope, local_sem.at[4]),
        pltpu.make_async_copy(rope_hbm, rope, local_sem.at[5]),
    ]
    for at in (0, 4, 5):
        loads[at].start()

    barrier = pltpu.get_barrier_semaphore()
    partners = (
        [in_group(*away) for away in AWAY[1:]]
        + [along_y(d) for d in range(1, Y)]
        + [along_z(d) for d in range(1, Z)]
    )
    for partner in partners:
        pl.semaphore_signal(barrier, inc=1, device_id=partner, device_id_type=MESH)
    for at in (1, 2, 3):
        loads[at].start()

    def send(stage, source, target, device):
        pltpu.make_async_remote_copy(
            src_ref=source,
            dst_ref=target,
            send_sem=send_sem.at[stage],
            recv_sem=recv_sem.at[stage],
            device_id=device,
            device_id_type=MESH,
        ).start()

    def wait_all(sems, stage, buffer):
        slots = buffer.at[pl.ds(1, buffer.shape[0] - 1)]
        pltpu.make_async_copy(slots, slots, sems.at[stage]).wait()

    row16 = iota((16, 128), 0)
    even = (row16 & 1) == 0
    for at in (4, 5, 0):
        loads[at].wait()
    nope_rows = nope[0].astype(F32)
    rope_rows = rope[0].astype(F32)
    latent = jnp.zeros((16, 128), F32)
    rotary = jnp.zeros((16, DR), F32)
    for h in range(2):
        left = jnp.where(
            even,
            jnp.broadcast_to(nope_rows[0, h : h + 1, :], (16, DN)),
            jnp.broadcast_to(nope_rows[1, h : h + 1, :], (16, DN)),
        ).astype(BF16)
        lifted = dot(left, key_lift[h])
        for c in range(4):
            latent = jnp.where(
                (row16 >> 1) == 2 * c + h, lifted[:, 128 * c : 128 * (c + 1)], latent
            )
        for j in range(2):
            rotary = jnp.where(
                row16[:, :DR] == 2 * h + j,
                jnp.broadcast_to(rope_rows[j, h : h + 1, :], (16, DR)),
                rotary,
            )
    near_q[0, 0:16, :] = latent.astype(BF16)
    near_q[0, 16:32, :] = jnp.concatenate([rotary, jnp.zeros((16, 128 - DR), F32)], axis=1).astype(BF16)
    for part in range(2):
        cache[part, LAT + DR :, :] = jnp.zeros((128 - DR, cache.shape[2]), BF16)

    pl.semaphore_wait(barrier, len(partners))

    for d in farthest_first(Y):
        send(0, near_q.at[0], near_q.at[d], along_y(d))
    sibling_cache = cache.at[1, pl.ds(0, LAT + DR)]
    send(7, cache_hbm, sibling_cache, in_group(0, 1))

    r = iota((5 * ROWS, Y * 32), 0)
    k = iota((5 * ROWS, Y * 32), 1)
    i = r & (ROWS - 1)
    spread = one_where(k == (i >> 2) * 32 + (r >> ROWS_BITS) * 4 + (i & 3))
    r = iota((Y * 32, 5 * ROWS), 0)
    k = iota((Y * 32, 5 * ROWS), 1)
    place = r & 31
    gather = one_where(k == jnp.minimum(place >> 2, 4) * ROWS + (r >> 5) * 4 + (place & 3))
    wait_all(recv_sem, 0, near_q)
    rows = dot(spread, near_q[...].reshape(Y * 32, 128))
    for c in range(5):
        all_q[0, :, 128 * c : 128 * (c + 1)] = rows[ROWS * c : ROWS * (c + 1)].astype(BF16)

    for dx in farthest_first(X):
        send(1, all_q.at[0], all_q.at[dx], in_group(dx, 0))
    wait_all(send_sem, 0, near_q)

    loads[2].wait()
    span = Y * 2 * COLS
    for ax in range(X):
        low = ax * span // 128 * 128
        high = min(-(-(ax + 1) * span // 128) * 128, X * span)
        n = iota((high - low, 256), 0) + low
        lane = iota((1, 256), 1)
        to_core, to_y, column = lane >> 7, (y + ((lane & 127) >> 4)) & (Y - 1), lane & 15
        source = ((ax * Y + to_y) * 2 + to_core) * COLS + column
        source = jnp.where(column < COLS, source, -1)
        choose = one_where(n == source)
        placed[:, 256 * ax : 256 * (ax + 1)] = dot(weight[:, low:high], choose).astype(BF16)

    loads[1].wait()
    span = cache.shape[2]
    block = span // 2
    count = ROWS * X
    limit = lengths[0] - 1 + (iota((count, 1), 0) & 1)
    scale = LOG2E * (DN + DR) ** -0.5
    wait_all(recv_sem, 1, all_q)
    query = all_q[...].reshape(count, LAT + 128)
    tops, denominators, weighted = [], [], []
    for part in range(2):
        if part:
            pltpu.make_async_copy(sibling_cache, sibling_cache, recv_sem.at[7]).wait()
        owner = ctx if part == 0 else ctx + 1 - 2 * core
        for start in range(0, span, block):
            visible = iota((1, block), 1) + (owner * span + start) < limit
            keys = cache[part, :, start : start + block]
            scores = jnp.where(visible, dot(query, keys) * scale, LOWEST)
            top = jnp.max(scores, axis=1, keepdims=True)
            expo = jnp.exp2(scores - top)
            tops.append(top)
            denominators.append(jnp.sum(expo, axis=1, keepdims=True))
            weighted.append(
                lax.dot_general(
                    expo.astype(BF16), keys[0:LAT], (((1,), (1,)), ((), ())), preferred_element_type=F32
                )
            )
    top = functools.reduce(jnp.maximum, tops)
    factors = [jnp.exp2(t - top) for t in tops]
    denominator = functools.reduce(jnp.add, [f * d for f, d in zip(factors, denominators)])
    total = functools.reduce(jnp.add, [f * w for f, w in zip(factors, weighted)])
    part_out[:, :, 0:LAT] = (total / denominator).astype(BF16).reshape(X, ROWS, LAT)
    part_out[:, :, LAT:] = stat_tile(top + jnp.log2(denominator), count).reshape(X, ROWS, 128)
    for dx in farthest_first(X):
        send(2, part_out.at[dx], part_in.at[dx], in_group(X - dx, 0))
    wait_all(send_sem, 1, all_q)
    pltpu.make_async_copy(sibling_cache, sibling_cache, send_sem.at[7]).wait()

    loads[3].wait()
    wait_all(recv_sem, 2, part_in)
    held = [part_out[0]] + [part_in[dx] for dx in range(1, X)]
    total, stat = combine(
        [part[:, 0:LAT].astype(F32) for part in held], [read_stat(part[:, LAT:]) for part in held]
    )
    total = total.astype(BF16)
    stacked = jnp.concatenate(
        [total[:, 128 * c : 128 * (c + 1)] for c in range(4)] + [stat_tile(stat, ROWS)], axis=0
    )
    own_out[...] = dot(gather, stacked).astype(BF16).reshape(Y, 32, 128)

    for d in farthest_first(Y):
        send(3, own_out.at[d], own_in.at[d], along_y(Y - d))
    wait_all(send_sem, 2, part_in)
    r = iota((128, 16), 0)
    k = iota((128, 16), 1)
    to_row = r & 15
    block = r >> 4
    source = (block & 3) * 4 + (block >> 2) * 2 + (to_row & 1)
    pick = one_where(k == source)
    wait_all(recv_sem, 3, own_in)
    held = [own_out[0]] + [own_in[d] for d in range(1, Y)]
    latent_out, _ = combine(
        [part[0:16].astype(F32) for part in held], [read_stat(part[16:32]) for part in held]
    )
    picked = dot(pick, latent_out.astype(BF16)).astype(BF16)
    for h in range(2):
        wide = jnp.concatenate([picked[64 * h + 16 * c : 64 * h + 16 * (c + 1)] for c in range(4)], axis=1)
        heads[0, :, DV * h : DV * (h + 1)] = dot(wide, value_lift[h])[0:2].astype(BF16).astype(F32)

    for d in farthest_first(Z):
        send(4, heads.at[0], heads.at[d], along_z(d))
    wait_all(send_sem, 3, own_in)
    wait_all(recv_sem, 4, heads)
    every = jnp.concatenate([heads[d] for d in range(Z)], axis=0).astype(BF16)
    product = dot(every, placed[...])
    for g in range(G):
        for half in range(2):
            tile = product[8 * half : 8 * half + 8, 128 * g : 128 * (g + 1)]
            sums_out[g, :, half, :] = blocks_transposed(tile)

    plane = [(g, d) for g in range(G) for d in range(Y)][1:]
    distance = lambda at: min(AWAY[at[0]][0], X - AWAY[at[0]][0]) + min(at[1], Y - at[1])
    for g, d in sorted(plane, key=lambda at: -distance(at)):
        dx, dc = AWAY[g]
        to_x, to_core, to_y = (x + dx) & (X - 1), (core + dc) & 1, (y + d) & (Y - 1)
        target = (row, (to_x * Y + to_y) * 2 + to_core)
        send(5, sums_out.at[to_x * 2 + to_core, d], sums_in.at[g * Y + d], target)
    wait_all(send_sem, 4, heads)
    wait_all(recv_sem, 5, sums_in)
    total = functools.reduce(jnp.add, [sums_in[at] for at in range(1, G * Y)]) + sums_out[x * 2 + core, 0]
    for half in range(2):
        wide = jnp.broadcast_to(total[half : half + 1], (8, 128))
        wide = pltpu.roll(wide, 16, 1, stride=16, stride_axis=0)
        for at in range(8):
            sequence = (row - (4 * half + at // 2)) & (Z - 1)
            out[sequence, at % 2 : at % 2 + 1, :] = wide[7 - at : 8 - at, 0:COLS]
    wait_all(send_sem, 5, sums_in)


def on_device(nope_query, rope_query, key_lift, value_lift, out_weight, latent_cache, lengths):
    cache = latent_cache[0].T
    in_hbm = (nope_query, rope_query, key_lift, value_lift, out_weight, cache)
    span = cache.shape[1]
    vmem = pl.BlockSpec(memory_space=pltpu.VMEM)
    hbm = pl.BlockSpec(memory_space=pltpu.HBM)
    return pl.pallas_call(
        kernel,
        out_shape=jax.ShapeDtypeStruct((Z, 2, COLS), F32),
        in_specs=[pl.BlockSpec(memory_space=pltpu.SMEM)] + [hbm] * 6,
        out_specs=vmem,
        scratch_shapes=[
            pltpu.VMEM(nope_query.shape, BF16),
            pltpu.VMEM(rope_query.shape, BF16),
            pltpu.VMEM(key_lift.shape, BF16),
            pltpu.VMEM(value_lift.shape, BF16),
            pltpu.VMEM(out_weight.shape, BF16),
            pltpu.VMEM((2, LAT + 128, span), BF16),
            pltpu.VMEM((2 * DV, 128 * G), BF16),
            pltpu.VMEM((Y, 32, 128), BF16),
            pltpu.VMEM((X, ROWS, LAT + 128), BF16),
            pltpu.VMEM((X, ROWS, LAT + 128), BF16),
            pltpu.VMEM((X, ROWS, LAT + 128), BF16),
            pltpu.VMEM((Y, 32, 128), BF16),
            pltpu.VMEM((Y, 32, 128), BF16),
            pltpu.VMEM((Z, 2, 2 * DV), F32),
            pltpu.VMEM((G, Y, 2, 128), F32),
            pltpu.VMEM((G * Y, 2, 128), F32),
            pltpu.SemaphoreType.DMA((6,)),
            pltpu.SemaphoreType.DMA((8,)),
            pltpu.SemaphoreType.DMA((8,)),
        ],
        compiler_params=pltpu.CompilerParams(
            collective_id=0, has_side_effects=True, vmem_limit_bytes=32 << 20
        ),
        cost_estimate=pl.CostEstimate(flops=600_000_000, bytes_accessed=2_500_000, transcendentals=300_000),
    )(lengths, *(pltpu.with_memory_space_constraint(a, pltpu.HBM) for a in in_hbm))


def solution(mesh):
    in_specs = (
        P("rows", None, "ctx", None),
        P("rows", None, "ctx", None),
        P("ctx", None, None),
        P("ctx", None, None),
        P("ctx", "rows"),
        P("rows", "ctx", None),
        P("rows"),
    )
    out_specs = P(None, None, ("rows", "ctx"))
    return jax.shard_map(
        on_device, mesh=mesh, in_specs=in_specs, out_specs=out_specs, check_vma=False
    )
```

```python
import functools

import jax
import jax.numpy as jnp
from jax import lax
from jax.experimental import pallas as pl
from jax.experimental.pallas import tpu as pltpu
from jax.sharding import PartitionSpec as P

DN = 128
DR = 64
LAT = 512
DV = 128
X, Y, Z = 4, 8, 8
G = 2 * X
COLS = 14
LOG2E = 1.4426950408889634
LOWEST = -1e30

MESH = pl.DeviceIdType.MESH
F32 = jnp.float32
BF16 = jnp.bfloat16

AWAY = [(dx, dc) for dx in range(X) for dc in range(2)]
SAME = [(dx, dy) for dx in range(X) for dy in range(Y)]
N = len(SAME)


def iota(shape, axis):
    return lax.broadcasted_iota(jnp.int32, shape, axis)


def dot(a, b):
    return jnp.dot(a, b, preferred_element_type=F32)


def hops(d, n):
    return min(d, n - d)


def farthest_first(n):
    return sorted(range(1, n), key=lambda d: -hops(d, n))


def one_where(condition):
    return jnp.where(condition, 1.0, 0.0).astype(BF16)


def split_three(value):
    high = value.astype(BF16)
    rest = value - high.astype(F32)
    middle = rest.astype(BF16)
    low = (rest - middle.astype(F32)).astype(BF16)
    return high, middle, low


def blocks_transposed(tile):
    row, block = iota((8, 128), 0), iota((8, 128), 1) >> 4
    for step in (1, 2, 4):
        above = pltpu.roll(pltpu.roll(tile, 8 - step, 0), 16 * step, 1)
        below = pltpu.roll(pltpu.roll(tile, step, 0), 128 - 16 * step, 1)
        stays = (row & step) == (block & step)
        tile = jnp.where(stays, tile, jnp.where((row & step) == 0, above, below))
    return tile


def kernel(
    lengths,
    nope_hbm,
    rope_hbm,
    key_lift_hbm,
    value_lift_hbm,
    weight_hbm,
    cache_hbm,
    out,
    nope,
    rope,
    key_lift,
    value_lift,
    weight,
    cache,
    placed,
    latents,
    rotaries,
    part_out,
    part_in,
    stat_out,
    stat_in,
    heads,
    sums_out,
    sums_in,
    local_sem,
    send_sem,
    recv_sem,
):
    row = lax.axis_index("rows")
    ctx = lax.axis_index("ctx")
    core = ctx & 1
    y = (ctx >> 1) & (Y - 1)
    x = ctx >> Y.bit_length()

    def in_plane(dx, dy, dc=0):
        to_x, to_y, to_core = (x + dx) & (X - 1), (y + dy) & (Y - 1), (core + dc) & 1
        return (row, (to_x * Y + to_y) * 2 + to_core)

    def along_z(d):
        return ((row + d) & (Z - 1), ctx)

    loads = [
        pltpu.make_async_copy(key_lift_hbm, key_lift, local_sem.at[0]),
        pltpu.make_async_copy(cache_hbm, cache.at[0, pl.ds(0, LAT + DR)], local_sem.at[1]),
        pltpu.make_async_copy(weight_hbm, weight, local_sem.at[2]),
        pltpu.make_async_copy(value_lift_hbm, value_lift, local_sem.at[3]),
        pltpu.make_async_copy(nope_hbm, nope, local_sem.at[4]),
        pltpu.make_async_copy(rope_hbm, rope, local_sem.at[5]),
    ]
    for at in (0, 4, 5):
        loads[at].start()

    barrier = pltpu.get_barrier_semaphore()
    far = sorted(range(1, N), key=lambda at: -hops(SAME[at][0], X) - hops(SAME[at][1], Y))
    partners = (
        [in_plane(*SAME[at]) for at in far]
        + [along_z(d) for d in farthest_first(Z)]
        + [in_plane(0, 0, 1)]
    )
    for partner in partners:
        pl.semaphore_signal(barrier, inc=1, device_id=partner, device_id_type=MESH)
    for at in (1, 2, 3):
        loads[at].start()

    def send(stage, source, target, device):
        pltpu.make_async_remote_copy(
            src_ref=source,
            dst_ref=target,
            send_sem=send_sem.at[stage],
            recv_sem=recv_sem.at[stage],
            device_id=device,
            device_id_type=MESH,
        ).start()

    def wait_all(sems, stage, buffer):
        slots = buffer.at[pl.ds(1, buffer.shape[0] - 1)]
        pltpu.make_async_copy(slots, slots, sems.at[stage]).wait()

    row16 = iota((16, 128), 0)
    even = (row16 & 1) == 0
    for at in (4, 5, 0):
        loads[at].wait()
    nope_rows = nope[0].astype(F32)
    rope_rows = rope[0].astype(F32)
    for j in range(2):
        rotaries[0, j : j + 1, :] = jnp.concatenate([rope_rows[j, h : h + 1, :] for h in range(2)], axis=1)
    latent = jnp.zeros((16, 128), F32)
    for h in range(2):
        left = jnp.where(
            even,
            jnp.broadcast_to(nope_rows[0, h : h + 1, :], (16, DN)),
            jnp.broadcast_to(nope_rows[1, h : h + 1, :], (16, DN)),
        ).astype(BF16)
        lifted = dot(left, key_lift[h])
        for c in range(4):
            latent = jnp.where(
                (row16 >> 1) == 2 * c + h, lifted[:, 128 * c : 128 * (c + 1)], latent
            )
    latents[0] = latent.astype(BF16)
    for part in range(2):
        cache[part, LAT + DR :, :] = jnp.zeros((128 - DR, cache.shape[2]), BF16)

    pl.semaphore_wait(barrier, len(partners))

    for at in far:
        device = in_plane(*SAME[at])
        send(0, latents.at[0], latents.at[at], device)
        send(1, rotaries.at[0], rotaries.at[at], device)
    sibling_cache = cache.at[1, pl.ds(0, LAT + DR)]
    send(2, cache_hbm, sibling_cache, in_plane(0, 0, 1))

    loads[2].wait()
    span = Y * 2 * COLS
    for ax in range(X):
        low = ax * span // 128 * 128
        high = min(-(-(ax + 1) * span // 128) * 128, X * span)
        n = iota((high - low, 256), 0) + low
        lane = iota((1, 256), 1)
        to_core, to_y, column = lane >> 7, (y + ((lane & 127) >> 4)) & (Y - 1), lane & 15
        source = ((ax * Y + to_y) * 2 + to_core) * COLS + column
        source = jnp.where(column < COLS, source, -1)
        choose = one_where(n == source)
        placed[:, 256 * ax : 256 * (ax + 1)] = dot(weight[:, low:high], choose).astype(BF16)

    r, k = iota((128, 128), 0), iota((128, 128), 1)
    spread = one_where(k == ((r >> 2) & 7) * 16 + (r >> 5) * 4 + (r & 3))
    gather = one_where(r == ((k >> 2) & 7) * 16 + (k >> 5) * 4 + (k & 3))
    turn = one_where(iota((4 * N, 2 * N), 1) == (iota((4 * N, 2 * N), 0) >> 2) * 2 + (iota((4 * N, 2 * N), 0) & 1))
    by_slot = one_where(iota((N, 4 * N), 0) == iota((N, 4 * N), 1) >> 2)

    loads[1].wait()
    span = cache.shape[2]
    block = span // 2
    count = 4 * N
    limit = lengths[0] - 1 + (iota((count, 1), 0) & 1)
    scale = LOG2E * (DN + DR) ** -0.5
    wait_all(recv_sem, 0, latents)
    wait_all(recv_sem, 1, rotaries)
    pieces = [dot(spread, latents[8 * at : 8 * at + 8].reshape(128, 128)).astype(BF16) for at in range(N // 8)]
    pieces = [
        jnp.concatenate([piece[32 * c : 32 * (c + 1)] for piece in pieces], axis=0) for c in range(4)
    ]
    turned = dot(turn, rotaries[...].reshape(2 * N, 128).astype(BF16))
    second_head = (iota((count, 1), 0) & 2) > 0
    pieces.append(jnp.where(second_head, pltpu.roll(turned, DR, 1), turned).astype(BF16))
    query = jnp.concatenate(pieces, axis=1)
    tops, denominators, weighted = [], [], []
    for part in range(2):
        if part:
            pltpu.make_async_copy(sibling_cache, sibling_cache, recv_sem.at[2]).wait()
        owner = ctx if part == 0 else ctx + 1 - 2 * core
        for start in range(0, span, block):
            visible = iota((1, block), 1) + (owner * span + start) < limit
            keys = cache[part, :, start : start + block]
            scores = jnp.where(visible, dot(query, keys) * scale, LOWEST)
            top = jnp.max(scores, axis=1, keepdims=True)
            expo = jnp.exp2(scores - top)
            tops.append(top)
            denominators.append(jnp.sum(expo, axis=1, keepdims=True))
            weighted.append(
                lax.dot_general(
                    expo.astype(BF16), keys[0:LAT], (((1,), (1,)), ((), ())), preferred_element_type=F32
                )
            )
    top = functools.reduce(jnp.maximum, tops)
    factors = [jnp.exp2(t - top) for t in tops]
    denominator = functools.reduce(jnp.add, [f * d for f, d in zip(factors, denominators)])
    total = functools.reduce(jnp.add, [f * w for f, w in zip(factors, weighted)])
    total = (total / denominator).astype(BF16)
    for at in range(N // 8):
        rows = total[32 * at : 32 * at + 32]
        rows = jnp.concatenate([rows[:, 128 * c : 128 * (c + 1)] for c in range(4)], axis=0)
        part_out[8 * at : 8 * at + 8] = dot(gather, rows).astype(BF16).reshape(8, 16, 128)
    k, lane = iota((count, 128), 0), iota((count, 128), 1)
    stat = jnp.where((k & 3) == (lane & 3), top + jnp.log2(denominator), 0.0)
    stat_out[:, 0, :] = functools.reduce(jnp.add, [dot(by_slot, piece) for piece in split_three(stat)])

    for at in far:
        dx, dy = SAME[at]
        device = in_plane(X - dx, Y - dy)
        send(6, stat_out.at[at], stat_in.at[at], device)
        send(3, part_out.at[at], part_in.at[at], device)
    part_in[0] = part_out[0]
    stat_in[0] = stat_out[0]
    wait_all(send_sem, 0, latents)
    wait_all(send_sem, 1, rotaries)
    pltpu.make_async_copy(sibling_cache, sibling_cache, send_sem.at[2]).wait()
    loads[3].wait()
    r = iota((128, 16), 0)
    k = iota((128, 16), 1)
    to_row = r & 15
    block = r >> 4
    source = (block & 3) * 4 + (block >> 2) * 2 + (to_row & 1)
    pick = one_where(k == source)
    wait_all(recv_sem, 6, stat_in)
    stat = stat_in[:, 0, :]
    factor = jnp.exp2(stat - jnp.max(stat, axis=0, keepdims=True))
    factor = (factor / jnp.sum(factor, axis=0, keepdims=True)).T[0:16]
    wait_all(recv_sem, 3, part_in)
    latent_out = functools.reduce(
        jnp.add, [factor[:, at : at + 1] * part_in[at].astype(F32) for at in range(N)]
    )
    picked = dot(pick, latent_out.astype(BF16)).astype(BF16)
    for h in range(2):
        wide = jnp.concatenate([picked[64 * h + 16 * c : 64 * h + 16 * (c + 1)] for c in range(4)], axis=1)
        heads[0, :, DV * h : DV * (h + 1)] = dot(wide, value_lift[h])[0:2].astype(BF16).astype(F32)

    for d in farthest_first(Z):
        send(4, heads.at[0], heads.at[d], along_z(d))
    wait_all(send_sem, 3, part_in)
    wait_all(send_sem, 6, stat_in)
    wait_all(recv_sem, 4, heads)
    every = jnp.concatenate([heads[d] for d in range(Z)], axis=0).astype(BF16)
    product = dot(every, placed[...])
    for g in range(G):
        for half in range(2):
            tile = product[8 * half : 8 * half + 8, 128 * g : 128 * (g + 1)]
            sums_out[g, :, half, :] = blocks_transposed(tile)

    plane = [(g, d) for g in range(G) for d in range(Y)][1:]
    for g, d in sorted(plane, key=lambda at: -hops(AWAY[at[0]][0], X) - hops(at[1], Y)):
        dx, dc = AWAY[g]
        chunk = ((x + dx) & (X - 1)) * 2 + ((core + dc) & 1)
        send(5, sums_out.at[chunk, d], sums_in.at[g * Y + d], in_plane(dx, d, dc))
    wait_all(send_sem, 4, heads)
    wait_all(recv_sem, 5, sums_in)
    total = functools.reduce(jnp.add, [sums_in[at] for at in range(1, G * Y)]) + sums_out[x * 2 + core, 0]
    for half in range(2):
        wide = jnp.broadcast_to(total[half : half + 1], (8, 128))
        wide = pltpu.roll(wide, 16, 1, stride=16, stride_axis=0)
        for at in range(8):
            sequence = (row - (4 * half + at // 2)) & (Z - 1)
            out[sequence, at % 2 : at % 2 + 1, :] = wide[7 - at : 8 - at, 0:COLS]
    wait_all(send_sem, 5, sums_in)


def on_device(nope_query, rope_query, key_lift, value_lift, out_weight, latent_cache, lengths):
    cache = latent_cache[0].T
    in_hbm = (nope_query, rope_query, key_lift, value_lift, out_weight, cache)
    span = cache.shape[1]
    vmem = pl.BlockSpec(memory_space=pltpu.VMEM)
    hbm = pl.BlockSpec(memory_space=pltpu.HBM)
    return pl.pallas_call(
        kernel,
        out_shape=jax.ShapeDtypeStruct((Z, 2, COLS), F32),
        in_specs=[pl.BlockSpec(memory_space=pltpu.SMEM)] + [hbm] * 6,
        out_specs=vmem,
        scratch_shapes=[
            pltpu.VMEM(nope_query.shape, BF16),
            pltpu.VMEM(rope_query.shape, BF16),
            pltpu.VMEM(key_lift.shape, BF16),
            pltpu.VMEM(value_lift.shape, BF16),
            pltpu.VMEM(out_weight.shape, BF16),
            pltpu.VMEM((2, LAT + 128, span), BF16),
            pltpu.VMEM((2 * DV, 128 * G), BF16),
            pltpu.VMEM((N, 16, 128), BF16),
            pltpu.VMEM((N, 2, 128), F32),
            pltpu.VMEM((N, 16, 128), BF16),
            pltpu.VMEM((N, 16, 128), BF16),
            pltpu.VMEM((N, 1, 128), F32),
            pltpu.VMEM((N, 1, 128), F32),
            pltpu.VMEM((Z, 2, 2 * DV), F32),
            pltpu.VMEM((G, Y, 2, 128), F32),
            pltpu.VMEM((G * Y, 2, 128), F32),
            pltpu.SemaphoreType.DMA((6,)),
            pltpu.SemaphoreType.DMA((7,)),
            pltpu.SemaphoreType.DMA((7,)),
        ],
        compiler_params=pltpu.CompilerParams(
            collective_id=0, has_side_effects=True, vmem_limit_bytes=32 << 20
        ),
        cost_estimate=pl.CostEstimate(flops=600_000_000, bytes_accessed=2_500_000, transcendentals=300_000),
    )(lengths, *(pltpu.with_memory_space_constraint(a, pltpu.HBM) for a in in_hbm))


def solution(mesh):
    in_specs = (
        P("rows", None, "ctx", None),
        P("rows", None, "ctx", None),
        P("ctx", None, None),
        P("ctx", None, None),
        P("ctx", "rows"),
        P("rows", "ctx", None),
        P("rows"),
    )
    out_specs = P(None, None, ("rows", "ctx"))
    return jax.shard_map(
        on_device, mesh=mesh, in_specs=in_specs, out_specs=out_specs, check_vma=False
    )
```

```python
import functools

import jax
import jax.numpy as jnp
from jax import lax
from jax.experimental import pallas as pl
from jax.experimental.pallas import tpu as pltpu
from jax.sharding import PartitionSpec as P

DN = 128
DR = 64
LAT = 512
DV = 128
X, Y, Z = 4, 8, 8
G = 2 * X
COLS = 14
LOG2E = 1.4426950408889634
LOWEST = -1e30

MESH = pl.DeviceIdType.MESH
F32 = jnp.float32
BF16 = jnp.bfloat16

AWAY = [(dx, dc) for dx in range(X) for dc in range(2)]
SAME = [(dx, dy) for dx in range(X) for dy in range(Y)]
N = len(SAME)


def iota(shape, axis):
    return lax.broadcasted_iota(jnp.int32, shape, axis)


def dot(a, b):
    return jnp.dot(a, b, preferred_element_type=F32)


def hops(d, n):
    return min(d, n - d)


def farthest_first(n):
    return sorted(range(1, n), key=lambda d: -hops(d, n))


def one_where(condition):
    return jnp.where(condition, 1.0, 0.0).astype(BF16)


def split_three(value):
    high = value.astype(BF16)
    rest = value - high.astype(F32)
    middle = rest.astype(BF16)
    low = (rest - middle.astype(F32)).astype(BF16)
    return high, middle, low


def blocks_transposed(tile):
    row, block = iota((8, 128), 0), iota((8, 128), 1) >> 4
    for step in (1, 2, 4):
        above = pltpu.roll(pltpu.roll(tile, 8 - step, 0), 16 * step, 1)
        below = pltpu.roll(pltpu.roll(tile, step, 0), 128 - 16 * step, 1)
        stays = (row & step) == (block & step)
        tile = jnp.where(stays, tile, jnp.where((row & step) == 0, above, below))
    return tile


def kernel(
    lengths,
    nope_hbm,
    rope_hbm,
    key_lift_hbm,
    value_lift_hbm,
    weight_hbm,
    cache_hbm,
    out,
    nope,
    rope,
    key_lift,
    value_lift,
    weight,
    cache,
    placed,
    latents,
    rotaries,
    part_out,
    part_in,
    stat_out,
    stat_in,
    heads,
    sums_out,
    sums_in,
    local_sem,
    send_sem,
    recv_sem,
):
    row = lax.axis_index("rows")
    ctx = lax.axis_index("ctx")
    core = ctx & 1
    y = (ctx >> 1) & (Y - 1)
    x = ctx >> Y.bit_length()

    def in_plane(dx, dy, dc=0):
        to_x, to_y, to_core = (x + dx) & (X - 1), (y + dy) & (Y - 1), (core + dc) & 1
        return (row, (to_x * Y + to_y) * 2 + to_core)

    def along_z(d):
        return ((row + d) & (Z - 1), ctx)

    loads = [
        pltpu.make_async_copy(key_lift_hbm, key_lift, local_sem.at[0]),
        pltpu.make_async_copy(cache_hbm, cache.at[0, pl.ds(0, LAT + DR)], local_sem.at[1]),
        pltpu.make_async_copy(weight_hbm, weight, local_sem.at[2]),
        pltpu.make_async_copy(value_lift_hbm, value_lift, local_sem.at[3]),
        pltpu.make_async_copy(nope_hbm, nope, local_sem.at[4]),
        pltpu.make_async_copy(rope_hbm, rope, local_sem.at[5]),
    ]
    for at in (0, 4, 5):
        loads[at].start()

    barrier = pltpu.get_barrier_semaphore()
    far = sorted(range(1, N), key=lambda at: -hops(SAME[at][0], X) - hops(SAME[at][1], Y))
    partners = (
        [in_plane(*SAME[at]) for at in far]
        + [along_z(d) for d in farthest_first(Z)]
        + [in_plane(0, 0, 1)]
    )
    for partner in partners:
        pl.semaphore_signal(barrier, inc=1, device_id=partner, device_id_type=MESH)
    for at in (1, 2, 3):
        loads[at].start()

    def send(stage, source, target, device):
        pltpu.make_async_remote_copy(
            src_ref=source,
            dst_ref=target,
            send_sem=send_sem.at[stage],
            recv_sem=recv_sem.at[stage],
            device_id=device,
            device_id_type=MESH,
        ).start()

    def wait_all(sems, stage, buffer):
        slots = buffer.at[pl.ds(1, buffer.shape[0] - 1)]
        pltpu.make_async_copy(slots, slots, sems.at[stage]).wait()

    row16 = iota((16, 128), 0)
    even = (row16 & 1) == 0
    for at in (4, 5, 0):
        loads[at].wait()
    nope_rows = nope[0].astype(F32)
    rope_rows = rope[0].astype(F32)
    for j in range(2):
        rotaries[0, j : j + 1, :] = jnp.concatenate([rope_rows[j, h : h + 1, :] for h in range(2)], axis=1)
    latent = jnp.zeros((16, 128), F32)
    for h in range(2):
        left = jnp.where(
            even,
            jnp.broadcast_to(nope_rows[0, h : h + 1, :], (16, DN)),
            jnp.broadcast_to(nope_rows[1, h : h + 1, :], (16, DN)),
        ).astype(BF16)
        lifted = dot(left, key_lift[h])
        for c in range(4):
            latent = jnp.where(
                (row16 >> 1) == 2 * c + h, lifted[:, 128 * c : 128 * (c + 1)], latent
            )
    latents[0] = latent.astype(BF16)
    for part in range(2):
        cache[part, LAT + DR :, :] = jnp.zeros((128 - DR, cache.shape[2]), BF16)

    pl.semaphore_wait(barrier, len(partners))

    for at in far:
        device = in_plane(*SAME[at])
        send(0, latents.at[0], latents.at[at], device)
        send(1, rotaries.at[0], rotaries.at[at], device)
    sibling_cache = cache.at[1, pl.ds(0, LAT + DR)]
    send(2, cache_hbm, sibling_cache, in_plane(0, 0, 1))

    loads[2].wait()
    span = Y * 2 * COLS
    for ax in range(X):
        low = ax * span // 128 * 128
        high = min(-(-(ax + 1) * span // 128) * 128, X * span)
        n = iota((high - low, 256), 0) + low
        lane = iota((1, 256), 1)
        to_core, to_y, column = lane >> 7, (y + ((lane & 127) >> 4)) & (Y - 1), lane & 15
        source = ((ax * Y + to_y) * 2 + to_core) * COLS + column
        source = jnp.where(column < COLS, source, -1)
        choose = one_where(n == source)
        placed[:, 256 * ax : 256 * (ax + 1)] = dot(weight[:, low:high], choose).astype(BF16)

    r, k = iota((128, 128), 0), iota((128, 128), 1)
    spread = one_where(k == ((r >> 2) & 7) * 16 + (r >> 5) * 4 + (r & 3))
    gather = one_where(r == ((k >> 2) & 7) * 16 + (k >> 5) * 4 + (k & 3))
    turn = one_where(iota((4 * N, 2 * N), 1) == (iota((4 * N, 2 * N), 0) >> 2) * 2 + (iota((4 * N, 2 * N), 0) & 1))
    by_slot = one_where(iota((N, 4 * N), 0) == iota((N, 4 * N), 1) >> 2)

    loads[1].wait()
    span = cache.shape[2]
    block = span // 2
    count = 4 * N
    limit = lengths[0] - 1 + (iota((count, 1), 0) & 1)
    scale = LOG2E * (DN + DR) ** -0.5
    pltpu.make_async_copy(sibling_cache, sibling_cache, recv_sem.at[2]).wait()
    wait_all(recv_sem, 1, rotaries)
    wait_all(recv_sem, 0, latents)
    pieces = [dot(spread, latents[8 * at : 8 * at + 8].reshape(128, 128)).astype(BF16) for at in range(N // 8)]
    pieces = [
        jnp.concatenate([piece[32 * c : 32 * (c + 1)] for piece in pieces], axis=0) for c in range(4)
    ]
    turned = dot(turn, rotaries[...].reshape(2 * N, 128).astype(BF16))
    second_head = (iota((count, 1), 0) & 2) > 0
    pieces.append(jnp.where(second_head, pltpu.roll(turned, DR, 1), turned).astype(BF16))
    query = jnp.concatenate(pieces, axis=1)
    tops, denominators, weighted = [], [], []
    for part in range(2):
        owner = ctx if part == 0 else ctx + 1 - 2 * core
        for start in range(0, span, block):
            visible = iota((1, block), 1) + (owner * span + start) < limit
            keys = cache[part, :, start : start + block]
            scores = jnp.where(visible, dot(query, keys) * scale, LOWEST)
            top = jnp.max(scores, axis=1, keepdims=True)
            expo = jnp.exp2(scores - top)
            tops.append(top)
            denominators.append(jnp.sum(expo, axis=1, keepdims=True))
            weighted.append(
                lax.dot_general(
                    expo.astype(BF16), keys[0:LAT], (((1,), (1,)), ((), ())), preferred_element_type=F32
                )
            )
    top = functools.reduce(jnp.maximum, tops)
    factors = [jnp.exp2(t - top) for t in tops]
    denominator = functools.reduce(jnp.add, [f * d for f, d in zip(factors, denominators)])
    total = functools.reduce(jnp.add, [f * w for f, w in zip(factors, weighted)])
    total = (total * (1.0 / denominator)).astype(BF16)
    for at in range(N // 8):
        rows = total[32 * at : 32 * at + 32]
        rows = jnp.concatenate([rows[:, 128 * c : 128 * (c + 1)] for c in range(4)], axis=0)
        part_out[8 * at : 8 * at + 8] = dot(gather, rows).astype(BF16).reshape(8, 16, 128)
    k, lane = iota((count, 128), 0), iota((count, 128), 1)
    stat = jnp.where((k & 3) == (lane & 3), top + jnp.log2(denominator), 0.0)
    stat_out[:, 0, :] = functools.reduce(jnp.add, [dot(by_slot, piece) for piece in split_three(stat)])

    for at in far:
        dx, dy = SAME[at]
        device = in_plane(X - dx, Y - dy)
        send(6, stat_out.at[at], stat_in.at[at], device)
        send(3, part_out.at[at], part_in.at[at], device)
    part_in[0] = part_out[0]
    stat_in[0] = stat_out[0]
    wait_all(send_sem, 0, latents)
    wait_all(send_sem, 1, rotaries)
    pltpu.make_async_copy(sibling_cache, sibling_cache, send_sem.at[2]).wait()
    loads[3].wait()
    wait_all(recv_sem, 6, stat_in)
    stat = stat_in[:, 0, :]
    factor = jnp.exp2(stat - jnp.max(stat, axis=0, keepdims=True))
    factor = (factor * (1.0 / jnp.sum(factor, axis=0, keepdims=True))).T[0:16]
    wait_all(recv_sem, 3, part_in)
    latent_out = functools.reduce(
        jnp.add, [factor[:, at : at + 1] * part_in[at].astype(F32) for at in range(N)]
    )
    wide = jnp.concatenate([jnp.where(row16 >> 2 == c, latent_out, 0.0) for c in range(4)], axis=1).astype(BF16)
    for h in range(2):
        lifted = dot(wide, value_lift[h])
        lifted = lifted + pltpu.roll(lifted, 8, 0)
        lifted = lifted + pltpu.roll(lifted, 4, 0)
        heads[0, :, DV * h : DV * (h + 1)] = lifted[2 * h : 2 * h + 2].astype(BF16).astype(F32)

    for d in farthest_first(Z):
        send(4, heads.at[0], heads.at[d], along_z(d))
    wait_all(send_sem, 3, part_in)
    wait_all(send_sem, 6, stat_in)
    wait_all(recv_sem, 4, heads)
    every = jnp.concatenate([heads[d] for d in range(Z)], axis=0).astype(BF16)
    product = dot(every, placed[...])
    for g in range(G):
        for half in range(2):
            tile = product[8 * half : 8 * half + 8, 128 * g : 128 * (g + 1)]
            sums_out[g, :, half, :] = blocks_transposed(tile)

    plane = [(g, d) for g in range(G) for d in range(Y)][1:]
    for g, d in sorted(plane, key=lambda at: -hops(AWAY[at[0]][0], X) - hops(at[1], Y)):
        dx, dc = AWAY[g]
        chunk = ((x + dx) & (X - 1)) * 2 + ((core + dc) & 1)
        send(5, sums_out.at[chunk, d], sums_in.at[g * Y + d], in_plane(dx, d, dc))
    wait_all(send_sem, 4, heads)
    wait_all(recv_sem, 5, sums_in)
    total = functools.reduce(jnp.add, [sums_in[at] for at in range(1, G * Y)]) + sums_out[x * 2 + core, 0]
    for half in range(2):
        wide = jnp.broadcast_to(total[half : half + 1], (8, 128))
        wide = pltpu.roll(wide, 16, 1, stride=16, stride_axis=0)
        for at in range(8):
            sequence = (row - (4 * half + at // 2)) & (Z - 1)
            out[sequence, at % 2 : at % 2 + 1, :] = wide[7 - at : 8 - at, 0:COLS]
    wait_all(send_sem, 5, sums_in)


def on_device(nope_query, rope_query, key_lift, value_lift, out_weight, latent_cache, lengths):
    cache = latent_cache[0].T
    in_hbm = (nope_query, rope_query, key_lift, value_lift, out_weight, cache)
    span = cache.shape[1]
    vmem = pl.BlockSpec(memory_space=pltpu.VMEM)
    hbm = pl.BlockSpec(memory_space=pltpu.HBM)
    return pl.pallas_call(
        kernel,
        out_shape=jax.ShapeDtypeStruct((Z, 2, COLS), F32),
        in_specs=[pl.BlockSpec(memory_space=pltpu.SMEM)] + [hbm] * 6,
        out_specs=vmem,
        scratch_shapes=[
            pltpu.VMEM(nope_query.shape, BF16),
            pltpu.VMEM(rope_query.shape, BF16),
            pltpu.VMEM(key_lift.shape, BF16),
            pltpu.VMEM(value_lift.shape, BF16),
            pltpu.VMEM(out_weight.shape, BF16),
            pltpu.VMEM((2, LAT + 128, span), BF16),
            pltpu.VMEM((2 * DV, 128 * G), BF16),
            pltpu.VMEM((N, 16, 128), BF16),
            pltpu.VMEM((N, 2, 128), F32),
            pltpu.VMEM((N, 16, 128), BF16),
            pltpu.VMEM((N, 16, 128), BF16),
            pltpu.VMEM((N, 1, 128), F32),
            pltpu.VMEM((N, 1, 128), F32),
            pltpu.VMEM((Z, 2, 2 * DV), F32),
            pltpu.VMEM((G, Y, 2, 128), F32),
            pltpu.VMEM((G * Y, 2, 128), F32),
            pltpu.SemaphoreType.DMA((6,)),
            pltpu.SemaphoreType.DMA((7,)),
            pltpu.SemaphoreType.DMA((7,)),
        ],
        compiler_params=pltpu.CompilerParams(
            collective_id=0, has_side_effects=True, vmem_limit_bytes=32 << 20
        ),
        cost_estimate=pl.CostEstimate(flops=600_000_000, bytes_accessed=2_500_000, transcendentals=300_000),
    )(lengths, *(pltpu.with_memory_space_constraint(a, pltpu.HBM) for a in in_hbm))


def solution(mesh):
    in_specs = (
        P("rows", None, "ctx", None),
        P("rows", None, "ctx", None),
        P("ctx", None, None),
        P("ctx", None, None),
        P("ctx", "rows"),
        P("rows", "ctx", None),
        P("rows"),
    )
    out_specs = P(None, None, ("rows", "ctx"))
    return jax.shard_map(
        on_device, mesh=mesh, in_specs=in_specs, out_specs=out_specs, check_vma=False
    )
```

```python
import functools

import jax
import jax.numpy as jnp
from jax import lax
from jax.experimental import pallas as pl
from jax.experimental.pallas import tpu as pltpu
from jax.sharding import PartitionSpec as P

DN = 128
DR = 64
LAT = 512
DV = 128
X, Y, Z = 4, 8, 8
G = 2 * X
COLS = 14
LOG2E = 1.4426950408889634
LOWEST = -1e30

MESH = pl.DeviceIdType.MESH
F32 = jnp.float32
BF16 = jnp.bfloat16

AWAY = [(dx, dc) for dx in range(X) for dc in range(2)]
SAME = [(dx, dy) for dx in range(X) for dy in range(Y)]
N = len(SAME)


def iota(shape, axis):
    return lax.broadcasted_iota(jnp.int32, shape, axis)


def dot(a, b):
    return jnp.dot(a, b, preferred_element_type=F32)


def hops(d, n):
    return min(d, n - d)


def farthest_first(n):
    return sorted(range(1, n), key=lambda d: -hops(d, n))


def one_where(condition):
    return jnp.where(condition, 1.0, 0.0).astype(BF16)


def split_three(value):
    high = value.astype(BF16)
    rest = value - high.astype(F32)
    middle = rest.astype(BF16)
    low = (rest - middle.astype(F32)).astype(BF16)
    return high, middle, low


def blocks_transposed(tile):
    row, block = iota((8, 128), 0), iota((8, 128), 1) >> 4
    for step in (1, 2, 4):
        above = pltpu.roll(pltpu.roll(tile, 8 - step, 0), 16 * step, 1)
        below = pltpu.roll(pltpu.roll(tile, step, 0), 128 - 16 * step, 1)
        stays = (row & step) == (block & step)
        tile = jnp.where(stays, tile, jnp.where((row & step) == 0, above, below))
    return tile


def kernel(
    lengths,
    nope_hbm,
    rope_hbm,
    key_lift_hbm,
    value_lift_hbm,
    weight_hbm,
    cache_hbm,
    out,
    nope,
    rope,
    key_lift,
    value_lift,
    weight,
    cache,
    placed,
    latents,
    rotaries,
    part_out,
    part_in,
    stat_out,
    stat_in,
    heads,
    sums_out,
    sums_in,
    local_sem,
    send_sem,
    recv_sem,
):
    row = lax.axis_index("rows")
    ctx = lax.axis_index("ctx")
    core = ctx & 1
    y = (ctx >> 1) & (Y - 1)
    x = ctx >> Y.bit_length()

    def in_plane(dx, dy, dc=0):
        to_x, to_y, to_core = (x + dx) & (X - 1), (y + dy) & (Y - 1), (core + dc) & 1
        return (row, (to_x * Y + to_y) * 2 + to_core)

    def along_z(d):
        return ((row + d) & (Z - 1), ctx)

    loads = [
        pltpu.make_async_copy(key_lift_hbm, key_lift, local_sem.at[0]),
        pltpu.make_async_copy(cache_hbm, cache.at[0, pl.ds(0, LAT + DR)], local_sem.at[1]),
        pltpu.make_async_copy(weight_hbm, weight, local_sem.at[2]),
        pltpu.make_async_copy(value_lift_hbm, value_lift, local_sem.at[3]),
        pltpu.make_async_copy(nope_hbm, nope, local_sem.at[4]),
        pltpu.make_async_copy(rope_hbm, rope, local_sem.at[5]),
    ]
    for at in (0, 4, 5):
        loads[at].start()

    barrier = pltpu.get_barrier_semaphore()
    far = sorted(range(1, N), key=lambda at: -hops(SAME[at][0], X) - hops(SAME[at][1], Y))
    partners = (
        [in_plane(*SAME[at]) for at in far]
        + [along_z(d) for d in farthest_first(Z)]
        + [in_plane(0, 0, 1)]
    )
    for partner in partners:
        pl.semaphore_signal(barrier, inc=1, device_id=partner, device_id_type=MESH)
    for at in (1, 2, 3):
        loads[at].start()

    def send(stage, source, target, device):
        pltpu.make_async_remote_copy(
            src_ref=source,
            dst_ref=target,
            send_sem=send_sem.at[stage],
            recv_sem=recv_sem.at[stage],
            device_id=device,
            device_id_type=MESH,
        ).start()

    def wait_all(sems, stage, buffer):
        slots = buffer.at[pl.ds(1, buffer.shape[0] - 1)]
        pltpu.make_async_copy(slots, slots, sems.at[stage]).wait()

    row16 = iota((16, 128), 0)
    even = (row16 & 1) == 0
    for at in (4, 5, 0):
        loads[at].wait()
    nope_rows = nope[0].astype(F32)
    rope_rows = rope[0].astype(F32)
    for j in range(2):
        rotaries[0, j : j + 1, :] = jnp.concatenate([rope_rows[j, h : h + 1, :] for h in range(2)], axis=1)
    latent = jnp.zeros((16, 128), F32)
    for h in range(2):
        left = jnp.where(
            even,
            jnp.broadcast_to(nope_rows[0, h : h + 1, :], (16, DN)),
            jnp.broadcast_to(nope_rows[1, h : h + 1, :], (16, DN)),
        ).astype(BF16)
        lifted = dot(left, key_lift[h])
        for c in range(4):
            latent = jnp.where(
                (row16 >> 1) == 2 * c + h, lifted[:, 128 * c : 128 * (c + 1)], latent
            )
    latents[0] = latent.astype(BF16)
    for part in range(2):
        cache[part, LAT + DR :, :] = jnp.zeros((128 - DR, cache.shape[2]), BF16)

    pl.semaphore_wait(barrier, len(partners))

    sibling_cache = cache.at[1, pl.ds(0, LAT + DR)]
    quarter = (LAT + DR) // 4
    for start in range(0, LAT + DR, quarter):
        rows = pl.ds(start, quarter)
        send(2, cache_hbm.at[rows], cache.at[1, rows], in_plane(0, 0, 1))

    for at in far:
        device = in_plane(*SAME[at])
        send(0, latents.at[0], latents.at[at], device)
        send(1, rotaries.at[0], rotaries.at[at], device)

    loads[2].wait()
    span = Y * 2 * COLS
    for ax in range(X):
        low = ax * span // 128 * 128
        high = min(-(-(ax + 1) * span // 128) * 128, X * span)
        n = iota((high - low, 256), 0) + low
        lane = iota((1, 256), 1)
        to_core, to_y, column = lane >> 7, (y + ((lane & 127) >> 4)) & (Y - 1), lane & 15
        source = ((ax * Y + to_y) * 2 + to_core) * COLS + column
        source = jnp.where(column < COLS, source, -1)
        choose = one_where(n == source)
        placed[:, 256 * ax : 256 * (ax + 1)] = dot(weight[:, low:high], choose).astype(BF16)

    r, k = iota((128, 128), 0), iota((128, 128), 1)
    spread = one_where(k == ((r >> 2) & 7) * 16 + (r >> 5) * 4 + (r & 3))
    gather = one_where(r == ((k >> 2) & 7) * 16 + (k >> 5) * 4 + (k & 3))
    turn = one_where(iota((4 * N, 2 * N), 1) == (iota((4 * N, 2 * N), 0) >> 2) * 2 + (iota((4 * N, 2 * N), 0) & 1))
    by_slot = one_where(iota((N, 4 * N), 0) == iota((N, 4 * N), 1) >> 2)

    loads[1].wait()
    span = cache.shape[2]
    block = span // 2
    count = 4 * N
    limit = lengths[0] - 1 + (iota((count, 1), 0) & 1)
    scale = LOG2E * (DN + DR) ** -0.5
    pltpu.make_async_copy(sibling_cache, sibling_cache, recv_sem.at[2]).wait()
    wait_all(recv_sem, 1, rotaries)
    wait_all(recv_sem, 0, latents)
    pieces = [dot(spread, latents[8 * at : 8 * at + 8].reshape(128, 128)).astype(BF16) for at in range(N // 8)]
    pieces = [
        jnp.concatenate([piece[32 * c : 32 * (c + 1)] for piece in pieces], axis=0) for c in range(4)
    ]
    turned = dot(turn, rotaries[...].reshape(2 * N, 128).astype(BF16))
    second_head = (iota((count, 1), 0) & 2) > 0
    pieces.append(jnp.where(second_head, pltpu.roll(turned, DR, 1), turned).astype(BF16))
    query = jnp.concatenate(pieces, axis=1)
    tops, denominators, weighted = [], [], []
    for part in range(2):
        owner = ctx if part == 0 else ctx + 1 - 2 * core
        for start in range(0, span, block):
            visible = iota((1, block), 1) + (owner * span + start) < limit
            keys = cache[part, :, start : start + block]
            scores = jnp.where(visible, dot(query, keys) * scale, LOWEST)
            top = jnp.max(scores, axis=1, keepdims=True)
            expo = jnp.exp2(scores - top)
            tops.append(top)
            denominators.append(jnp.sum(expo, axis=1, keepdims=True))
            weighted.append(
                lax.dot_general(
                    expo.astype(BF16), keys[0:LAT], (((1,), (1,)), ((), ())), preferred_element_type=F32
                )
            )
    top = functools.reduce(jnp.maximum, tops)
    factors = [jnp.exp2(t - top) for t in tops]
    denominator = functools.reduce(jnp.add, [f * d for f, d in zip(factors, denominators)])
    total = functools.reduce(jnp.add, [f * w for f, w in zip(factors, weighted)])
    total = (total * (1.0 / denominator)).astype(BF16)
    for at in range(N // 8):
        rows = total[32 * at : 32 * at + 32]
        rows = jnp.concatenate([rows[:, 128 * c : 128 * (c + 1)] for c in range(4)], axis=0)
        part_out[8 * at : 8 * at + 8] = dot(gather, rows).astype(BF16).reshape(8, 16, 128)
    k, lane = iota((count, 128), 0), iota((count, 128), 1)
    stat = jnp.where((k & 3) == (lane & 3), top + jnp.log2(denominator), 0.0)
    stat_out[:, 0, :] = functools.reduce(jnp.add, [dot(by_slot, piece) for piece in split_three(stat)])

    for at in far:
        dx, dy = SAME[at]
        device = in_plane(X - dx, Y - dy)
        send(6, stat_out.at[at], stat_in.at[at], device)
        send(3, part_out.at[at], part_in.at[at], device)
    part_in[0] = part_out[0]
    stat_in[0] = stat_out[0]
    wait_all(send_sem, 0, latents)
    wait_all(send_sem, 1, rotaries)
    pltpu.make_async_copy(sibling_cache, sibling_cache, send_sem.at[2]).wait()
    loads[3].wait()
    wait_all(recv_sem, 6, stat_in)
    stat = stat_in[:, 0, :]
    factor = jnp.exp2(stat - jnp.max(stat, axis=0, keepdims=True))
    factor = (factor * (1.0 / jnp.sum(factor, axis=0, keepdims=True))).T[0:16]
    wait_all(recv_sem, 3, part_in)
    latent_out = functools.reduce(
        jnp.add, [factor[:, at : at + 1] * part_in[at].astype(F32) for at in range(N)]
    )
    wide = jnp.concatenate([jnp.where(row16 >> 2 == c, latent_out, 0.0) for c in range(4)], axis=1).astype(BF16)
    for h in range(2):
        lifted = dot(wide, value_lift[h])
        lifted = lifted + pltpu.roll(lifted, 8, 0)
        lifted = lifted + pltpu.roll(lifted, 4, 0)
        heads[0, :, DV * h : DV * (h + 1)] = lifted[2 * h : 2 * h + 2].astype(BF16).astype(F32)

    for d in farthest_first(Z):
        send(4, heads.at[0], heads.at[d], along_z(d))
    wait_all(send_sem, 3, part_in)
    wait_all(send_sem, 6, stat_in)
    wait_all(recv_sem, 4, heads)
    every = jnp.concatenate([heads[d] for d in range(Z)], axis=0).astype(BF16)
    product = dot(every, placed[...])
    for g in range(G):
        for half in range(2):
            tile = product[8 * half : 8 * half + 8, 128 * g : 128 * (g + 1)]
            sums_out[g, :, half, :] = blocks_transposed(tile)

    plane = [(g, d) for g in range(G) for d in range(Y)][1:]
    for g, d in sorted(plane, key=lambda at: -hops(AWAY[at[0]][0], X) - hops(at[1], Y)):
        dx, dc = AWAY[g]
        chunk = ((x + dx) & (X - 1)) * 2 + ((core + dc) & 1)
        send(5, sums_out.at[chunk, d], sums_in.at[g * Y + d], in_plane(dx, d, dc))
    wait_all(send_sem, 4, heads)
    wait_all(recv_sem, 5, sums_in)
    total = functools.reduce(jnp.add, [sums_in[at] for at in range(1, G * Y)]) + sums_out[x * 2 + core, 0]
    for half in range(2):
        wide = jnp.broadcast_to(total[half : half + 1], (8, 128))
        wide = pltpu.roll(wide, 16, 1, stride=16, stride_axis=0)
        for at in range(8):
            sequence = (row - (4 * half + at // 2)) & (Z - 1)
            out[sequence, at % 2 : at % 2 + 1, :] = wide[7 - at : 8 - at, 0:COLS]
    wait_all(send_sem, 5, sums_in)


def on_device(nope_query, rope_query, key_lift, value_lift, out_weight, latent_cache, lengths):
    cache = latent_cache[0].T
    in_hbm = (nope_query, rope_query, key_lift, value_lift, out_weight, cache)
    span = cache.shape[1]
    vmem = pl.BlockSpec(memory_space=pltpu.VMEM)
    hbm = pl.BlockSpec(memory_space=pltpu.HBM)
    return pl.pallas_call(
        kernel,
        out_shape=jax.ShapeDtypeStruct((Z, 2, COLS), F32),
        in_specs=[pl.BlockSpec(memory_space=pltpu.SMEM)] + [hbm] * 6,
        out_specs=vmem,
        scratch_shapes=[
            pltpu.VMEM(nope_query.shape, BF16),
            pltpu.VMEM(rope_query.shape, BF16),
            pltpu.VMEM(key_lift.shape, BF16),
            pltpu.VMEM(value_lift.shape, BF16),
            pltpu.VMEM(out_weight.shape, BF16),
            pltpu.VMEM((2, LAT + 128, span), BF16),
            pltpu.VMEM((2 * DV, 128 * G), BF16),
            pltpu.VMEM((N, 16, 128), BF16),
            pltpu.VMEM((N, 2, 128), F32),
            pltpu.VMEM((N, 16, 128), BF16),
            pltpu.VMEM((N, 16, 128), BF16),
            pltpu.VMEM((N, 1, 128), F32),
            pltpu.VMEM((N, 1, 128), F32),
            pltpu.VMEM((Z, 2, 2 * DV), F32),
            pltpu.VMEM((G, Y, 2, 128), F32),
            pltpu.VMEM((G * Y, 2, 128), F32),
            pltpu.SemaphoreType.DMA((6,)),
            pltpu.SemaphoreType.DMA((7,)),
            pltpu.SemaphoreType.DMA((7,)),
        ],
        compiler_params=pltpu.CompilerParams(
            collective_id=0, has_side_effects=True, vmem_limit_bytes=32 << 20
        ),
        cost_estimate=pl.CostEstimate(flops=600_000_000, bytes_accessed=2_500_000, transcendentals=300_000),
    )(lengths, *(pltpu.with_memory_space_constraint(a, pltpu.HBM) for a in in_hbm))


def solution(mesh):
    in_specs = (
        P("rows", None, "ctx", None),
        P("rows", None, "ctx", None),
        P("ctx", None, None),
        P("ctx", None, None),
        P("ctx", "rows"),
        P("rows", "ctx", None),
        P("rows"),
    )
    out_specs = P(None, None, ("rows", "ctx"))
    return jax.shard_map(
        on_device, mesh=mesh, in_specs=in_specs, out_specs=out_specs, check_vma=False
    )
```

```python
import functools

import jax
import jax.numpy as jnp
from jax import lax
from jax.experimental import pallas as pl
from jax.experimental.pallas import tpu as pltpu
from jax.sharding import PartitionSpec as P

DN = 128
DR = 64
LAT = 512
DV = 128
X, Y, Z = 4, 8, 8
G = 2 * X
COLS = 14
LOG2E = 1.4426950408889634
LOWEST = -1e30

MESH = pl.DeviceIdType.MESH
F32 = jnp.float32
BF16 = jnp.bfloat16

AWAY = [(dx, dc) for dx in range(X) for dc in range(2)]
SAME = [(dx, dy) for dx in range(X) for dy in range(Y)]
N = len(SAME)
ROWS = 4 * Y
HALVES = ((2, 3), (1, 0))


def iota(shape, axis):
    return lax.broadcasted_iota(jnp.int32, shape, axis)


def dot(a, b):
    return jnp.dot(a, b, preferred_element_type=F32)


def hops(d, n):
    return min(d, n - d)


def farthest_first(n):
    return sorted(range(1, n), key=lambda d: -hops(d, n))


def one_where(condition):
    return jnp.where(condition, 1.0, 0.0).astype(BF16)


def split_three(value):
    high = value.astype(BF16)
    rest = value - high.astype(F32)
    middle = rest.astype(BF16)
    low = (rest - middle.astype(F32)).astype(BF16)
    return high, middle, low


def blocks_transposed(tile):
    row, block = iota((8, 128), 0), iota((8, 128), 1) >> 4
    for step in (1, 2, 4):
        above = pltpu.roll(pltpu.roll(tile, 8 - step, 0), 16 * step, 1)
        below = pltpu.roll(pltpu.roll(tile, step, 0), 128 - 16 * step, 1)
        stays = (row & step) == (block & step)
        tile = jnp.where(stays, tile, jnp.where((row & step) == 0, above, below))
    return tile


def kernel(
    lengths,
    nope_hbm,
    rope_hbm,
    key_lift_hbm,
    value_lift_hbm,
    weight_hbm,
    cache_hbm,
    out,
    nope,
    rope,
    key_lift,
    value_lift,
    weight,
    cache,
    placed,
    latents,
    rotaries,
    part_out,
    part_in,
    stat_out,
    stat_in,
    heads,
    sums_out,
    sums_in,
    local_sem,
    send_sem,
    recv_sem,
):
    row = lax.axis_index("rows")
    ctx = lax.axis_index("ctx")
    core = ctx & 1
    y = (ctx >> 1) & (Y - 1)
    x = ctx >> Y.bit_length()

    def in_plane(dx, dy, dc=0):
        to_x, to_y, to_core = (x + dx) & (X - 1), (y + dy) & (Y - 1), (core + dc) & 1
        return (row, (to_x * Y + to_y) * 2 + to_core)

    def along_z(d):
        return ((row + d) & (Z - 1), ctx)

    loads = [
        pltpu.make_async_copy(key_lift_hbm, key_lift, local_sem.at[0]),
        pltpu.make_async_copy(cache_hbm, cache.at[0, pl.ds(0, LAT + DR)], local_sem.at[1]),
        pltpu.make_async_copy(weight_hbm, weight, local_sem.at[2]),
        pltpu.make_async_copy(value_lift_hbm, value_lift, local_sem.at[3]),
        pltpu.make_async_copy(nope_hbm, nope, local_sem.at[4]),
        pltpu.make_async_copy(rope_hbm, rope, local_sem.at[5]),
    ]
    for at in (0, 4, 5):
        loads[at].start()

    barrier = pltpu.get_barrier_semaphore()
    far = sorted(range(1, N), key=lambda at: -hops(SAME[at][0], X) - hops(SAME[at][1], Y))
    halves = [[at for at in far if SAME[at][0] in half] for half in HALVES]
    partners = (
        [in_plane(*SAME[at]) for at in far]
        + [along_z(d) for d in farthest_first(Z)]
        + [in_plane(0, 0, 1)]
    )
    for partner in partners:
        pl.semaphore_signal(barrier, inc=1, device_id=partner, device_id_type=MESH)
    for at in (1, 2, 3):
        loads[at].start()

    def send(stage, source, target, device):
        pltpu.make_async_remote_copy(
            src_ref=source,
            dst_ref=target,
            send_sem=send_sem.at[stage],
            recv_sem=recv_sem.at[stage],
            device_id=device,
            device_id_type=MESH,
        ).start()

    def wait_all(sems, stage, buffer, count=None):
        slots = buffer.at[pl.ds(1, buffer.shape[0] - 1 if count is None else count)]
        pltpu.make_async_copy(slots, slots, sems.at[stage]).wait()

    row16 = iota((16, 128), 0)
    even = (row16 & 1) == 0
    for at in (4, 5, 0):
        loads[at].wait()
    nope_rows = nope[0].astype(F32)
    rope_rows = rope[0].astype(F32)
    for j in range(2):
        rotaries[0, j : j + 1, :] = jnp.concatenate([rope_rows[j, h : h + 1, :] for h in range(2)], axis=1)
    latent = jnp.zeros((16, 128), F32)
    for h in range(2):
        left = jnp.where(
            even,
            jnp.broadcast_to(nope_rows[0, h : h + 1, :], (16, DN)),
            jnp.broadcast_to(nope_rows[1, h : h + 1, :], (16, DN)),
        ).astype(BF16)
        lifted = dot(left, key_lift[h])
        for c in range(4):
            latent = jnp.where(
                (row16 >> 1) == 2 * c + h, lifted[:, 128 * c : 128 * (c + 1)], latent
            )
    latents[0] = latent.astype(BF16)
    for part in range(2):
        cache[part, LAT + DR :, :] = jnp.zeros((128 - DR, cache.shape[2]), BF16)

    pl.semaphore_wait(barrier, len(partners))

    sibling_cache = cache.at[1, pl.ds(0, LAT + DR)]
    quarter = (LAT + DR) // 4
    for start in range(0, LAT + DR, quarter):
        rows = pl.ds(start, quarter)
        send(2, cache_hbm.at[rows], cache.at[1, rows], in_plane(0, 0, 1))

    for half, slots in enumerate(halves):
        for at in slots:
            device = in_plane(*SAME[at])
            send(7 + half, latents.at[0], latents.at[at], device)
            send(half, rotaries.at[0], rotaries.at[at], device)

    loads[2].wait()
    span = Y * 2 * COLS
    for ax in range(X):
        low = ax * span // 128 * 128
        high = min(-(-(ax + 1) * span // 128) * 128, X * span)
        n = iota((high - low, 256), 0) + low
        lane = iota((1, 256), 1)
        to_core, to_y, column = lane >> 7, (y + ((lane & 127) >> 4)) & (Y - 1), lane & 15
        source = ((ax * Y + to_y) * 2 + to_core) * COLS + column
        source = jnp.where(column < COLS, source, -1)
        choose = one_where(n == source)
        placed[:, 256 * ax : 256 * (ax + 1)] = dot(weight[:, low:high], choose).astype(BF16)

    count = 2 * ROWS
    r, k = iota((128, 128), 0), iota((128, 128), 1)
    spread = one_where(k == ((r >> 2) & 7) * 16 + (r >> 5) * 4 + (r & 3))
    gather = one_where(r == ((k >> 2) & 7) * 16 + (k >> 5) * 4 + (k & 3))
    r, k = iota((ROWS, 2 * Y), 0), iota((ROWS, 2 * Y), 1)
    turn = one_where(k == (r >> 2) * 2 + (r & 1))
    second_head = (iota((ROWS, 1), 0) & 2) > 0
    r, k = iota((2 * Y, count), 0), iota((2 * Y, count), 1)
    by_slot = one_where(r == k >> 2)

    loads[1].wait()
    span = cache.shape[2]
    limit = lengths[0] - 1 + (iota((count, 1), 0) & 1)
    scale = LOG2E * (DN + DR) ** -0.5
    pltpu.make_async_copy(sibling_cache, sibling_cache, recv_sem.at[2]).wait()
    for half, (slots, at_x) in enumerate(zip(halves, HALVES)):
        wait_all(recv_sem, half, rotaries, len(slots))
        wait_all(recv_sem, 7 + half, latents, len(slots))
        query = []
        for dx in at_x:
            rows = dot(spread, latents[Y * dx : Y * (dx + 1)].reshape(128, 128)).astype(BF16)
            rotary = dot(turn, rotaries[Y * dx : Y * (dx + 1)].reshape(2 * Y, 128).astype(BF16))
            rotary = jnp.where(second_head, pltpu.roll(rotary, DR, 1), rotary).astype(BF16)
            rows = [rows[ROWS * c : ROWS * (c + 1)] for c in range(4)]
            query.append(jnp.concatenate(rows + [rotary], axis=1))
        query = jnp.concatenate(query, axis=0)
        tops, denominators, weighted = [], [], []
        for part in range(2):
            owner = ctx if part == 0 else ctx + 1 - 2 * core
            visible = iota((1, span), 1) + owner * span < limit
            scores = jnp.where(visible, dot(query, cache[part]) * scale, LOWEST)
            top = jnp.max(scores, axis=1, keepdims=True)
            expo = jnp.exp2(scores - top)
            tops.append(top)
            denominators.append(jnp.sum(expo, axis=1, keepdims=True))
            weighted.append(
                lax.dot_general(
                    expo.astype(BF16), cache[part, 0:LAT, :], (((1,), (1,)), ((), ())), preferred_element_type=F32
                )
            )
        top = jnp.maximum(tops[0], tops[1])
        factors = [jnp.exp2(t - top) for t in tops]
        denominator = factors[0] * denominators[0] + factors[1] * denominators[1]
        inverse = 1.0 / denominator
        total = (weighted[0] * (factors[0] * inverse) + weighted[1] * (factors[1] * inverse)).astype(BF16)
        for at, dx in enumerate(at_x):
            rows = total[ROWS * at : ROWS * (at + 1)]
            rows = jnp.concatenate([rows[:, 128 * c : 128 * (c + 1)] for c in range(4)], axis=0)
            part_out[Y * dx : Y * (dx + 1)] = dot(gather, rows).astype(BF16).reshape(Y, 16, 128)
        k, lane = iota((count, 128), 0), iota((count, 128), 1)
        stat = jnp.where((k & 3) == (lane & 3), top + jnp.log2(denominator), 0.0)
        stat = functools.reduce(jnp.add, [dot(by_slot, piece) for piece in split_three(stat)])
        for at, dx in enumerate(at_x):
            stat_out[Y * dx : Y * (dx + 1), 0, :] = stat[Y * at : Y * (at + 1)]

        for at in slots:
            dx, dy = SAME[at]
            device = in_plane(X - dx, Y - dy)
            send(6, stat_out.at[at], stat_in.at[at], device)
            send(3, part_out.at[at], part_in.at[at], device)
    part_in[0] = part_out[0]
    stat_in[0] = stat_out[0]
    for half, slots in enumerate(halves):
        wait_all(send_sem, half, rotaries, len(slots))
        wait_all(send_sem, 7 + half, latents, len(slots))
    pltpu.make_async_copy(sibling_cache, sibling_cache, send_sem.at[2]).wait()
    loads[3].wait()
    wait_all(recv_sem, 6, stat_in)
    stat = stat_in[:, 0, :]
    factor = jnp.exp2(stat - jnp.max(stat, axis=0, keepdims=True))
    factor = (factor * (1.0 / jnp.sum(factor, axis=0, keepdims=True))).T[0:16]
    wait_all(recv_sem, 3, part_in)
    latent_out = functools.reduce(
        jnp.add, [factor[:, at : at + 1] * part_in[at].astype(F32) for at in range(N)]
    )
    wide = jnp.concatenate([jnp.where(row16 >> 2 == c, latent_out, 0.0) for c in range(4)], axis=1).astype(BF16)
    for h in range(2):
        lifted = dot(wide, value_lift[h])
        lifted = lifted + pltpu.roll(lifted, 8, 0)
        lifted = lifted + pltpu.roll(lifted, 4, 0)
        heads[0, :, DV * h : DV * (h + 1)] = lifted[2 * h : 2 * h + 2].astype(BF16).astype(F32)

    for d in farthest_first(Z):
        send(4, heads.at[0], heads.at[d], along_z(d))
    wait_all(send_sem, 3, part_in)
    wait_all(send_sem, 6, stat_in)
    wait_all(recv_sem, 4, heads)
    every = jnp.concatenate([heads[d] for d in range(Z)], axis=0).astype(BF16)
    product = dot(every, placed[...])
    for g in range(G):
        for half in range(2):
            tile = product[8 * half : 8 * half + 8, 128 * g : 128 * (g + 1)]
            sums_out[g, :, half, :] = blocks_transposed(tile)

    plane = [(g, d) for g in range(G) for d in range(Y)][1:]
    for g, d in sorted(plane, key=lambda at: -hops(AWAY[at[0]][0], X) - hops(at[1], Y)):
        dx, dc = AWAY[g]
        chunk = ((x + dx) & (X - 1)) * 2 + ((core + dc) & 1)
        send(5, sums_out.at[chunk, d], sums_in.at[g * Y + d], in_plane(dx, d, dc))
    wait_all(send_sem, 4, heads)
    wait_all(recv_sem, 5, sums_in)
    total = functools.reduce(jnp.add, [sums_in[at] for at in range(1, G * Y)]) + sums_out[x * 2 + core, 0]
    for half in range(2):
        wide = jnp.broadcast_to(total[half : half + 1], (8, 128))
        wide = pltpu.roll(wide, 16, 1, stride=16, stride_axis=0)
        for at in range(8):
            sequence = (row - (4 * half + at // 2)) & (Z - 1)
            out[sequence, at % 2 : at % 2 + 1, :] = wide[7 - at : 8 - at, 0:COLS]
    wait_all(send_sem, 5, sums_in)


def on_device(nope_query, rope_query, key_lift, value_lift, out_weight, latent_cache, lengths):
    cache = latent_cache[0].T
    in_hbm = (nope_query, rope_query, key_lift, value_lift, out_weight, cache)
    span = cache.shape[1]
    vmem = pl.BlockSpec(memory_space=pltpu.VMEM)
    hbm = pl.BlockSpec(memory_space=pltpu.HBM)
    return pl.pallas_call(
        kernel,
        out_shape=jax.ShapeDtypeStruct((Z, 2, COLS), F32),
        in_specs=[pl.BlockSpec(memory_space=pltpu.SMEM)] + [hbm] * 6,
        out_specs=vmem,
        scratch_shapes=[
            pltpu.VMEM(nope_query.shape, BF16),
            pltpu.VMEM(rope_query.shape, BF16),
            pltpu.VMEM(key_lift.shape, BF16),
            pltpu.VMEM(value_lift.shape, BF16),
            pltpu.VMEM(out_weight.shape, BF16),
            pltpu.VMEM((2, LAT + 128, span), BF16),
            pltpu.VMEM((2 * DV, 128 * G), BF16),
            pltpu.VMEM((N, 16, 128), BF16),
            pltpu.VMEM((N, 2, 128), F32),
            pltpu.VMEM((N, 16, 128), BF16),
            pltpu.VMEM((N, 16, 128), BF16),
            pltpu.VMEM((N, 1, 128), F32),
            pltpu.VMEM((N, 1, 128), F32),
            pltpu.VMEM((Z, 2, 2 * DV), F32),
            pltpu.VMEM((G, Y, 2, 128), F32),
            pltpu.VMEM((G * Y, 2, 128), F32),
            pltpu.SemaphoreType.DMA((6,)),
            pltpu.SemaphoreType.DMA((9,)),
            pltpu.SemaphoreType.DMA((9,)),
        ],
        compiler_params=pltpu.CompilerParams(
            collective_id=0, has_side_effects=True, vmem_limit_bytes=32 << 20
        ),
        cost_estimate=pl.CostEstimate(flops=600_000_000, bytes_accessed=2_500_000, transcendentals=300_000),
    )(lengths, *(pltpu.with_memory_space_constraint(a, pltpu.HBM) for a in in_hbm))


def solution(mesh):
    in_specs = (
        P("rows", None, "ctx", None),
        P("rows", None, "ctx", None),
        P("ctx", None, None),
        P("ctx", None, None),
        P("ctx", "rows"),
        P("rows", "ctx", None),
        P("rows"),
    )
    out_specs = P(None, None, ("rows", "ctx"))
    return jax.shard_map(
        on_device, mesh=mesh, in_specs=in_specs, out_specs=out_specs, check_vma=False
    )
```

```python
import functools

import jax
import jax.numpy as jnp
from jax import lax
from jax.experimental import pallas as pl
from jax.experimental.pallas import tpu as pltpu
from jax.sharding import PartitionSpec as P

DN = 128
DR = 64
LAT = 512
DV = 128
X, Y, Z = 4, 8, 8
G = 2 * X
COLS = 14
LOG2E = 1.4426950408889634
LOWEST = -1e30

MESH = pl.DeviceIdType.MESH
F32 = jnp.float32
BF16 = jnp.bfloat16

AWAY = [(dx, dc) for dx in range(X) for dc in range(2)]
SAME = [(dx, dy) for dx in range(X) for dy in range(Y)]
N = len(SAME)


def iota(shape, axis):
    return lax.broadcasted_iota(jnp.int32, shape, axis)


def dot(a, b):
    return jnp.dot(a, b, preferred_element_type=F32)


def hops(d, n):
    return min(d, n - d)


def farthest_first(n):
    return sorted(range(1, n), key=lambda d: -hops(d, n))


def dot_last(a, b):
    return lax.dot_general(a, b, (((1,), (1,)), ((), ())), preferred_element_type=F32)


def one_where(condition):
    return jnp.where(condition, 1.0, 0.0).astype(BF16)


def split_three(value):
    high = value.astype(BF16)
    rest = value - high.astype(F32)
    middle = rest.astype(BF16)
    low = (rest - middle.astype(F32)).astype(BF16)
    return high, middle, low


def blocks_transposed(tile):
    row, block = iota((8, 128), 0), iota((8, 128), 1) >> 4
    for step in (1, 2, 4):
        above = pltpu.roll(pltpu.roll(tile, 8 - step, 0), 16 * step, 1)
        below = pltpu.roll(pltpu.roll(tile, step, 0), 128 - 16 * step, 1)
        stays = (row & step) == (block & step)
        tile = jnp.where(stays, tile, jnp.where((row & step) == 0, above, below))
    return tile


def kernel(
    lengths,
    nope_hbm,
    rope_hbm,
    key_lift_hbm,
    value_lift_hbm,
    weight_hbm,
    cache_hbm,
    out,
    nope,
    rope,
    key_lift,
    value_lift,
    weight,
    cache,
    placed,
    latents,
    rotaries,
    part_out,
    part_in,
    stat_out,
    stat_in,
    heads,
    sums_out,
    sums_in,
    local_sem,
    send_sem,
    recv_sem,
):
    row = lax.axis_index("rows")
    ctx = lax.axis_index("ctx")
    core = ctx & 1
    y = (ctx >> 1) & (Y - 1)
    x = ctx >> Y.bit_length()

    def in_plane(dx, dy, dc=0):
        to_x, to_y, to_core = (x + dx) & (X - 1), (y + dy) & (Y - 1), (core + dc) & 1
        return (row, (to_x * Y + to_y) * 2 + to_core)

    def along_z(d):
        return ((row + d) & (Z - 1), ctx)

    loads = [
        pltpu.make_async_copy(key_lift_hbm, key_lift, local_sem.at[0]),
        pltpu.make_async_copy(cache_hbm, cache.at[0, pl.ds(0, LAT + DR)], local_sem.at[1]),
        pltpu.make_async_copy(weight_hbm, weight, local_sem.at[2]),
        pltpu.make_async_copy(value_lift_hbm, value_lift, local_sem.at[3]),
        pltpu.make_async_copy(nope_hbm, nope, local_sem.at[4]),
        pltpu.make_async_copy(rope_hbm, rope, local_sem.at[5]),
    ]
    for at in (0, 4, 5):
        loads[at].start()

    barrier = pltpu.get_barrier_semaphore()
    far = sorted(range(1, N), key=lambda at: -hops(SAME[at][0], X) - hops(SAME[at][1], Y))
    partners = (
        [in_plane(*SAME[at]) for at in far]
        + [along_z(d) for d in farthest_first(Z)]
        + [in_plane(0, 0, 1)]
    )
    for partner in partners:
        pl.semaphore_signal(barrier, inc=1, device_id=partner, device_id_type=MESH)
    for at in (1, 2, 3):
        loads[at].start()

    def send(stage, source, target, device):
        pltpu.make_async_remote_copy(
            src_ref=source,
            dst_ref=target,
            send_sem=send_sem.at[stage],
            recv_sem=recv_sem.at[stage],
            device_id=device,
            device_id_type=MESH,
        ).start()

    def wait_all(sems, stage, buffer):
        slots = buffer.at[pl.ds(1, buffer.shape[0] - 1)]
        pltpu.make_async_copy(slots, slots, sems.at[stage]).wait()

    row16 = iota((16, 128), 0)
    even = (row16 & 1) == 0
    for at in (4, 5, 0):
        loads[at].wait()
    nope_rows = nope[0].astype(F32)
    rope_rows = rope[0].astype(F32)
    for j in range(2):
        rotaries[0, j : j + 1, :] = jnp.concatenate([rope_rows[j, h : h + 1, :] for h in range(2)], axis=1)
    latent = jnp.zeros((16, 128), F32)
    for h in range(2):
        left = jnp.where(
            even,
            jnp.broadcast_to(nope_rows[0, h : h + 1, :], (16, DN)),
            jnp.broadcast_to(nope_rows[1, h : h + 1, :], (16, DN)),
        ).astype(BF16)
        lifted = dot(left, key_lift[h])
        for c in range(4):
            latent = jnp.where(
                (row16 >> 1) == 2 * c + h, lifted[:, 128 * c : 128 * (c + 1)], latent
            )
    latents[0] = latent.astype(BF16)
    for part in range(2):
        cache[part, LAT + DR :, :] = jnp.zeros((128 - DR, cache.shape[2]), BF16)

    pl.semaphore_wait(barrier, len(partners))

    sibling_cache = cache.at[1, pl.ds(0, LAT + DR)]
    quarter = (LAT + DR) // 4
    for start in range(0, LAT + DR, quarter):
        rows = pl.ds(start, quarter)
        send(2, cache_hbm.at[rows], cache.at[1, rows], in_plane(0, 0, 1))

    for at in far:
        device = in_plane(*SAME[at])
        send(0, latents.at[0], latents.at[at], device)
        send(1, rotaries.at[0], rotaries.at[at], device)

    loads[2].wait()
    span = Y * 2 * COLS
    for ax in range(X):
        low = ax * span // 128 * 128
        high = min(-(-(ax + 1) * span // 128) * 128, X * span)
        n = iota((high - low, 256), 0) + low
        lane = iota((1, 256), 1)
        to_core, to_y, column = lane >> 7, (y + ((lane & 127) >> 4)) & (Y - 1), lane & 15
        source = ((ax * Y + to_y) * 2 + to_core) * COLS + column
        source = jnp.where(column < COLS, source, -1)
        choose = one_where(n == source)
        placed[:, 256 * ax : 256 * (ax + 1)] = dot(weight[:, low:high], choose).astype(BF16)

    r, k = iota((128, 128), 0), iota((128, 128), 1)
    spread = one_where(k == ((r >> 2) & 7) * 16 + (r >> 5) * 4 + (r & 3))
    r, k = iota((16 * N, 16 * N), 0), iota((16 * N, 16 * N), 1)
    gather = one_where(k == ((r >> 2) & 3) * 4 * N + (r >> 4) * 4 + (r & 3))
    turn = one_where(iota((4 * N, 2 * N), 1) == (iota((4 * N, 2 * N), 0) >> 2) * 2 + (iota((4 * N, 2 * N), 0) & 1))
    by_slot = one_where(iota((N, 4 * N), 0) == iota((N, 4 * N), 1) >> 2)

    loads[1].wait()
    span = cache.shape[2]
    count = 4 * N
    limit = lengths[0] - 1 + (iota((count, 1), 0) & 1)
    scale = LOG2E * (DN + DR) ** -0.5
    pltpu.make_async_copy(sibling_cache, sibling_cache, recv_sem.at[2]).wait()
    wait_all(recv_sem, 1, rotaries)
    wait_all(recv_sem, 0, latents)
    pieces = [dot(spread, latents[8 * at : 8 * at + 8].reshape(128, 128)).astype(BF16) for at in range(N // 8)]
    pieces = [
        jnp.concatenate([piece[32 * c : 32 * (c + 1)] for piece in pieces], axis=0) for c in range(4)
    ]
    turned = dot(turn, rotaries[...].reshape(2 * N, 128).astype(BF16))
    second_head = (iota((count, 1), 0) & 2) > 0
    pieces.append(jnp.where(second_head, pltpu.roll(turned, DR, 1), turned).astype(BF16))
    query = jnp.concatenate(pieces, axis=1)
    scores = []
    for part in range(2):
        owner = ctx if part == 0 else ctx + 1 - 2 * core
        visible = iota((1, span), 1) + owner * span < limit
        scores.append(jnp.where(visible, dot(query, cache[part]) * scale, LOWEST))
    top = jnp.max(jnp.maximum(scores[0], scores[1]), axis=1, keepdims=True)
    expos = [jnp.exp2(score - top) for score in scores]
    denominator = jnp.sum(expos[0] + expos[1], axis=1, keepdims=True)
    inverse = 1.0 / denominator
    turned = functools.reduce(
        jnp.add, [dot_last(cache[part, 0:LAT, :], (expos[part] * inverse).astype(BF16)) for part in range(2)]
    ).astype(BF16)
    rows = jnp.concatenate([turned[128 * c : 128 * (c + 1)] for c in range(4)], axis=1)
    part_out[...] = dot_last(gather, rows).astype(BF16).reshape(N, 16, 128)
    k, lane = iota((count, 128), 0), iota((count, 128), 1)
    stat = jnp.where((k & 3) == (lane & 3), top + jnp.log2(denominator), 0.0)
    stat_out[:, 0, :] = functools.reduce(jnp.add, [dot(by_slot, piece) for piece in split_three(stat)])

    for at in far:
        dx, dy = SAME[at]
        device = in_plane(X - dx, Y - dy)
        send(6, stat_out.at[at], stat_in.at[at], device)
        send(3, part_out.at[at], part_in.at[at], device)
    part_in[0] = part_out[0]
    stat_in[0] = stat_out[0]
    wait_all(send_sem, 0, latents)
    wait_all(send_sem, 1, rotaries)
    pltpu.make_async_copy(sibling_cache, sibling_cache, send_sem.at[2]).wait()
    loads[3].wait()
    wait_all(recv_sem, 6, stat_in)
    stat = stat_in[:, 0, :]
    factor = jnp.exp2(stat - jnp.max(stat, axis=0, keepdims=True))
    factor = (factor * (1.0 / jnp.sum(factor, axis=0, keepdims=True))).T[0:16]
    wait_all(recv_sem, 3, part_in)
    latent_out = functools.reduce(
        jnp.add, [factor[:, at : at + 1] * part_in[at].astype(F32) for at in range(N)]
    )
    wide = jnp.concatenate([jnp.where(row16 >> 2 == c, latent_out, 0.0) for c in range(4)], axis=1).astype(BF16)
    for h in range(2):
        lifted = dot(wide, value_lift[h])
        lifted = lifted + pltpu.roll(lifted, 8, 0)
        lifted = lifted + pltpu.roll(lifted, 4, 0)
        heads[0, :, DV * h : DV * (h + 1)] = lifted[2 * h : 2 * h + 2].astype(BF16).astype(F32)

    for d in farthest_first(Z):
        send(4, heads.at[0], heads.at[d], along_z(d))
    wait_all(send_sem, 3, part_in)
    wait_all(send_sem, 6, stat_in)
    wait_all(recv_sem, 4, heads)
    every = jnp.concatenate([heads[d] for d in range(Z)], axis=0).astype(BF16)
    product = dot(every, placed[...])
    for g in range(G):
        for half in range(2):
            tile = product[8 * half : 8 * half + 8, 128 * g : 128 * (g + 1)]
            sums_out[g, :, half, :] = blocks_transposed(tile)

    plane = [(g, d) for g in range(G) for d in range(Y)][1:]
    for g, d in sorted(plane, key=lambda at: -hops(AWAY[at[0]][0], X) - hops(at[1], Y)):
        dx, dc = AWAY[g]
        chunk = ((x + dx) & (X - 1)) * 2 + ((core + dc) & 1)
        send(5, sums_out.at[chunk, d], sums_in.at[g * Y + d], in_plane(dx, d, dc))
    wait_all(send_sem, 4, heads)
    wait_all(recv_sem, 5, sums_in)
    total = functools.reduce(jnp.add, [sums_in[at] for at in range(1, G * Y)]) + sums_out[x * 2 + core, 0]
    for half in range(2):
        wide = jnp.broadcast_to(total[half : half + 1], (8, 128))
        wide = pltpu.roll(wide, 16, 1, stride=16, stride_axis=0)
        for at in range(8):
            sequence = (row - (4 * half + at // 2)) & (Z - 1)
            out[sequence, at % 2 : at % 2 + 1, :] = wide[7 - at : 8 - at, 0:COLS]
    wait_all(send_sem, 5, sums_in)


def on_device(nope_query, rope_query, key_lift, value_lift, out_weight, latent_cache, lengths):
    cache = latent_cache[0].T
    in_hbm = (nope_query, rope_query, key_lift, value_lift, out_weight, cache)
    span = cache.shape[1]
    vmem = pl.BlockSpec(memory_space=pltpu.VMEM)
    hbm = pl.BlockSpec(memory_space=pltpu.HBM)
    return pl.pallas_call(
        kernel,
        out_shape=jax.ShapeDtypeStruct((Z, 2, COLS), F32),
        in_specs=[pl.BlockSpec(memory_space=pltpu.SMEM)] + [hbm] * 6,
        out_specs=vmem,
        scratch_shapes=[
            pltpu.VMEM(nope_query.shape, BF16),
            pltpu.VMEM(rope_query.shape, BF16),
            pltpu.VMEM(key_lift.shape, BF16),
            pltpu.VMEM(value_lift.shape, BF16),
            pltpu.VMEM(out_weight.shape, BF16),
            pltpu.VMEM((2, LAT + 128, span), BF16),
            pltpu.VMEM((2 * DV, 128 * G), BF16),
            pltpu.VMEM((N, 16, 128), BF16),
            pltpu.VMEM((N, 2, 128), F32),
            pltpu.VMEM((N, 16, 128), BF16),
            pltpu.VMEM((N, 16, 128), BF16),
            pltpu.VMEM((N, 1, 128), F32),
            pltpu.VMEM((N, 1, 128), F32),
            pltpu.VMEM((Z, 2, 2 * DV), F32),
            pltpu.VMEM((G, Y, 2, 128), F32),
            pltpu.VMEM((G * Y, 2, 128), F32),
            pltpu.SemaphoreType.DMA((6,)),
            pltpu.SemaphoreType.DMA((7,)),
            pltpu.SemaphoreType.DMA((7,)),
        ],
        compiler_params=pltpu.CompilerParams(
            collective_id=0, has_side_effects=True, vmem_limit_bytes=32 << 20
        ),
        cost_estimate=pl.CostEstimate(flops=600_000_000, bytes_accessed=2_500_000, transcendentals=300_000),
    )(lengths, *(pltpu.with_memory_space_constraint(a, pltpu.HBM) for a in in_hbm))


def solution(mesh):
    in_specs = (
        P("rows", None, "ctx", None),
        P("rows", None, "ctx", None),
        P("ctx", None, None),
        P("ctx", None, None),
        P("ctx", "rows"),
        P("rows", "ctx", None),
        P("rows"),
    )
    out_specs = P(None, None, ("rows", "ctx"))
    return jax.shard_map(
        on_device, mesh=mesh, in_specs=in_specs, out_specs=out_specs, check_vma=False
    )
```

```python
import functools

import jax
import jax.numpy as jnp
from jax import lax
from jax.experimental import pallas as pl
from jax.experimental.pallas import tpu as pltpu
from jax.sharding import PartitionSpec as P

DN = 128
DR = 64
LAT = 512
DV = 128
X, Y, Z = 4, 8, 8
G = 2 * X
COLS = 14
LOG2E = 1.4426950408889634
LOWEST = -1e30

MESH = pl.DeviceIdType.MESH
F32 = jnp.float32
BF16 = jnp.bfloat16

AWAY = [(dx, dc) for dx in range(X) for dc in range(2)]
SAME = [(dx, dy) for dx in range(X) for dy in range(Y)]
N = len(SAME)
RELAYED = (4, 3, 5)


def iota(shape, axis):
    return lax.broadcasted_iota(jnp.int32, shape, axis)


def dot(a, b):
    return jnp.dot(a, b, preferred_element_type=F32)


def hops(d, n):
    return min(d, n - d)


def farthest_first(n):
    return sorted(range(1, n), key=lambda d: -hops(d, n))


def one_where(condition):
    return jnp.where(condition, 1.0, 0.0).astype(BF16)


def split_three(value):
    high = value.astype(BF16)
    rest = value - high.astype(F32)
    middle = rest.astype(BF16)
    low = (rest - middle.astype(F32)).astype(BF16)
    return high, middle, low


def blocks_transposed(tile):
    row, block = iota((8, 128), 0), iota((8, 128), 1) >> 4
    for step in (1, 2, 4):
        above = pltpu.roll(pltpu.roll(tile, 8 - step, 0), 16 * step, 1)
        below = pltpu.roll(pltpu.roll(tile, step, 0), 128 - 16 * step, 1)
        stays = (row & step) == (block & step)
        tile = jnp.where(stays, tile, jnp.where((row & step) == 0, above, below))
    return tile


def kernel(
    lengths,
    nope_hbm,
    rope_hbm,
    key_lift_hbm,
    value_lift_hbm,
    weight_hbm,
    cache_hbm,
    out,
    nope,
    rope,
    key_lift,
    value_lift,
    weight,
    cache,
    placed,
    latents,
    rotaries,
    part_out,
    part_in,
    stat_out,
    stat_in,
    heads,
    sums_out,
    sums_in,
    local_sem,
    send_sem,
    recv_sem,
):
    row = lax.axis_index("rows")
    ctx = lax.axis_index("ctx")
    core = ctx & 1
    y = (ctx >> 1) & (Y - 1)
    x = ctx >> Y.bit_length()

    def in_plane(dx, dy, dc=0):
        to_x, to_y, to_core = (x + dx) & (X - 1), (y + dy) & (Y - 1), (core + dc) & 1
        return (row, (to_x * Y + to_y) * 2 + to_core)

    def along_z(d):
        return ((row + d) & (Z - 1), ctx)

    loads = [
        pltpu.make_async_copy(key_lift_hbm, key_lift, local_sem.at[0]),
        pltpu.make_async_copy(cache_hbm, cache.at[0, pl.ds(0, LAT + DR)], local_sem.at[1]),
        pltpu.make_async_copy(weight_hbm, weight, local_sem.at[2]),
        pltpu.make_async_copy(value_lift_hbm, value_lift, local_sem.at[3]),
        pltpu.make_async_copy(nope_hbm, nope, local_sem.at[4]),
        pltpu.make_async_copy(rope_hbm, rope, local_sem.at[5]),
    ]
    for at in (0, 4, 5):
        loads[at].start()

    barrier = pltpu.get_barrier_semaphore()
    far = sorted(range(1, N), key=lambda at: -hops(SAME[at][0], X) - hops(SAME[at][1], Y))
    direct = [at for at in far if SAME[at][0] == 0 or SAME[at][1] not in RELAYED]
    partners = (
        [in_plane(*SAME[at]) for at in direct]
        + [along_z(d) for d in farthest_first(Z)]
        + [in_plane(0, 0, 1)]
    )
    for partner in partners:
        pl.semaphore_signal(barrier, inc=1, device_id=partner, device_id_type=MESH)
    for at in (1, 2, 3):
        loads[at].start()

    def send(stage, source, target, device):
        pltpu.make_async_remote_copy(
            src_ref=source,
            dst_ref=target,
            send_sem=send_sem.at[stage],
            recv_sem=recv_sem.at[stage],
            device_id=device,
            device_id_type=MESH,
        ).start()

    def wait_all(sems, stage, buffer, count=None):
        slots = buffer.at[pl.ds(1, buffer.shape[0] - 1 if count is None else count)]
        pltpu.make_async_copy(slots, slots, sems.at[stage]).wait()

    row16 = iota((16, 128), 0)
    even = (row16 & 1) == 0
    for at in (4, 5, 0):
        loads[at].wait()
    nope_rows = nope[0].astype(F32)
    rope_rows = rope[0].astype(F32)
    for j in range(2):
        rotaries[0, j : j + 1, :] = jnp.concatenate([rope_rows[j, h : h + 1, :] for h in range(2)], axis=1)
    latent = jnp.zeros((16, 128), F32)
    for h in range(2):
        left = jnp.where(
            even,
            jnp.broadcast_to(nope_rows[0, h : h + 1, :], (16, DN)),
            jnp.broadcast_to(nope_rows[1, h : h + 1, :], (16, DN)),
        ).astype(BF16)
        lifted = dot(left, key_lift[h])
        for c in range(4):
            latent = jnp.where(
                (row16 >> 1) == 2 * c + h, lifted[:, 128 * c : 128 * (c + 1)], latent
            )
    latents[0] = latent.astype(BF16)
    for part in range(2):
        cache[part, LAT + DR :, :] = jnp.zeros((128 - DR, cache.shape[2]), BF16)

    pl.semaphore_wait(barrier, len(partners))

    sibling_cache = cache.at[1, pl.ds(0, LAT + DR)]
    quarter = (LAT + DR) // 4
    for start in range(0, LAT + DR, quarter):
        rows = pl.ds(start, quarter)
        send(2, cache_hbm.at[rows], cache.at[1, rows], in_plane(0, 0, 1))

    for at, dy in enumerate(RELAYED):
        send(7 + at, latents.at[0], latents.at[dy], in_plane(0, dy))
        send(10 + at, rotaries.at[0], rotaries.at[dy], in_plane(0, dy))
    for at in direct:
        if at not in RELAYED:
            device = in_plane(*SAME[at])
            send(0, latents.at[0], latents.at[at], device)
            send(1, rotaries.at[0], rotaries.at[at], device)
    for at, dy in enumerate(RELAYED):
        wait_all(recv_sem, 7 + at, latents, 1)
        wait_all(recv_sem, 10 + at, rotaries, 1)
        for dx in farthest_first(X):
            send(0, latents.at[dy], latents.at[Y * dx + dy], in_plane(dx, 0))
            send(1, rotaries.at[dy], rotaries.at[Y * dx + dy], in_plane(dx, 0))
    others = N - 1 - len(RELAYED)

    loads[2].wait()
    span = Y * 2 * COLS
    for ax in range(X):
        low = ax * span // 128 * 128
        high = min(-(-(ax + 1) * span // 128) * 128, X * span)
        n = iota((high - low, 256), 0) + low
        lane = iota((1, 256), 1)
        to_core, to_y, column = lane >> 7, (y + ((lane & 127) >> 4)) & (Y - 1), lane & 15
        source = ((ax * Y + to_y) * 2 + to_core) * COLS + column
        source = jnp.where(column < COLS, source, -1)
        choose = one_where(n == source)
        placed[:, 256 * ax : 256 * (ax + 1)] = dot(weight[:, low:high], choose).astype(BF16)

    r, k = iota((128, 128), 0), iota((128, 128), 1)
    spread = one_where(k == ((r >> 2) & 7) * 16 + (r >> 5) * 4 + (r & 3))
    gather = one_where(r == ((k >> 2) & 7) * 16 + (k >> 5) * 4 + (k & 3))
    turn = one_where(iota((4 * N, 2 * N), 1) == (iota((4 * N, 2 * N), 0) >> 2) * 2 + (iota((4 * N, 2 * N), 0) & 1))
    by_slot = one_where(iota((N, 4 * N), 0) == iota((N, 4 * N), 1) >> 2)

    loads[1].wait()
    span = cache.shape[2]
    block = span // 2
    count = 4 * N
    limit = lengths[0] - 1 + (iota((count, 1), 0) & 1)
    scale = LOG2E * (DN + DR) ** -0.5
    pltpu.make_async_copy(sibling_cache, sibling_cache, recv_sem.at[2]).wait()
    wait_all(recv_sem, 1, rotaries, others)
    wait_all(recv_sem, 0, latents, others)
    pieces = [dot(spread, latents[8 * at : 8 * at + 8].reshape(128, 128)).astype(BF16) for at in range(N // 8)]
    pieces = [
        jnp.concatenate([piece[32 * c : 32 * (c + 1)] for piece in pieces], axis=0) for c in range(4)
    ]
    turned = dot(turn, rotaries[...].reshape(2 * N, 128).astype(BF16))
    second_head = (iota((count, 1), 0) & 2) > 0
    pieces.append(jnp.where(second_head, pltpu.roll(turned, DR, 1), turned).astype(BF16))
    query = jnp.concatenate(pieces, axis=1)
    tops, denominators, weighted = [], [], []
    for part in range(2):
        owner = ctx if part == 0 else ctx + 1 - 2 * core
        for start in range(0, span, block):
            visible = iota((1, block), 1) + (owner * span + start) < limit
            keys = cache[part, :, start : start + block]
            scores = jnp.where(visible, dot(query, keys) * scale, LOWEST)
            top = jnp.max(scores, axis=1, keepdims=True)
            expo = jnp.exp2(scores - top)
            tops.append(top)
            denominators.append(jnp.sum(expo, axis=1, keepdims=True))
            weighted.append(
                lax.dot_general(
                    expo.astype(BF16), keys[0:LAT], (((1,), (1,)), ((), ())), preferred_element_type=F32
                )
            )
    top = functools.reduce(jnp.maximum, tops)
    factors = [jnp.exp2(t - top) for t in tops]
    denominator = functools.reduce(jnp.add, [f * d for f, d in zip(factors, denominators)])
    total = functools.reduce(jnp.add, [f * w for f, w in zip(factors, weighted)])
    total = (total * (1.0 / denominator)).astype(BF16)
    for at in range(N // 8):
        rows = total[32 * at : 32 * at + 32]
        rows = jnp.concatenate([rows[:, 128 * c : 128 * (c + 1)] for c in range(4)], axis=0)
        part_out[8 * at : 8 * at + 8] = dot(gather, rows).astype(BF16).reshape(8, 16, 128)
    k, lane = iota((count, 128), 0), iota((count, 128), 1)
    stat = jnp.where((k & 3) == (lane & 3), top + jnp.log2(denominator), 0.0)
    stat_out[:, 0, :] = functools.reduce(jnp.add, [dot(by_slot, piece) for piece in split_three(stat)])

    for at in far:
        dx, dy = SAME[at]
        device = in_plane(X - dx, Y - dy)
        send(6, stat_out.at[at], stat_in.at[at], device)
        send(3, part_out.at[at], part_in.at[at], device)
    part_in[0] = part_out[0]
    stat_in[0] = stat_out[0]
    wait_all(send_sem, 0, latents, others)
    wait_all(send_sem, 1, rotaries, others)
    for at in range(len(RELAYED)):
        wait_all(send_sem, 7 + at, latents, 1)
        wait_all(send_sem, 10 + at, rotaries, 1)
    pltpu.make_async_copy(sibling_cache, sibling_cache, send_sem.at[2]).wait()
    loads[3].wait()
    wait_all(recv_sem, 6, stat_in)
    stat = stat_in[:, 0, :]
    factor = jnp.exp2(stat - jnp.max(stat, axis=0, keepdims=True))
    factor = (factor * (1.0 / jnp.sum(factor, axis=0, keepdims=True))).T[0:16]
    wait_all(recv_sem, 3, part_in)
    latent_out = functools.reduce(
        jnp.add, [factor[:, at : at + 1] * part_in[at].astype(F32) for at in range(N)]
    )
    wide = jnp.concatenate([jnp.where(row16 >> 2 == c, latent_out, 0.0) for c in range(4)], axis=1).astype(BF16)
    for h in range(2):
        lifted = dot(wide, value_lift[h])
        lifted = lifted + pltpu.roll(lifted, 8, 0)
        lifted = lifted + pltpu.roll(lifted, 4, 0)
        heads[0, :, DV * h : DV * (h + 1)] = lifted[2 * h : 2 * h + 2].astype(BF16).astype(F32)

    for d in farthest_first(Z):
        send(4, heads.at[0], heads.at[d], along_z(d))
    wait_all(send_sem, 3, part_in)
    wait_all(send_sem, 6, stat_in)
    wait_all(recv_sem, 4, heads)
    every = jnp.concatenate([heads[d] for d in range(Z)], axis=0).astype(BF16)
    product = dot(every, placed[...])
    for g in range(G):
        for half in range(2):
            tile = product[8 * half : 8 * half + 8, 128 * g : 128 * (g + 1)]
            sums_out[g, :, half, :] = blocks_transposed(tile)

    plane = [(g, d) for g in range(G) for d in range(Y)][1:]
    for g, d in sorted(plane, key=lambda at: -hops(AWAY[at[0]][0], X) - hops(at[1], Y)):
        dx, dc = AWAY[g]
        chunk = ((x + dx) & (X - 1)) * 2 + ((core + dc) & 1)
        send(5, sums_out.at[chunk, d], sums_in.at[g * Y + d], in_plane(dx, d, dc))
    wait_all(send_sem, 4, heads)
    wait_all(recv_sem, 5, sums_in)
    total = functools.reduce(jnp.add, [sums_in[at] for at in range(1, G * Y)]) + sums_out[x * 2 + core, 0]
    for half in range(2):
        wide = jnp.broadcast_to(total[half : half + 1], (8, 128))
        wide = pltpu.roll(wide, 16, 1, stride=16, stride_axis=0)
        for at in range(8):
            sequence = (row - (4 * half + at // 2)) & (Z - 1)
            out[sequence, at % 2 : at % 2 + 1, :] = wide[7 - at : 8 - at, 0:COLS]
    wait_all(send_sem, 5, sums_in)


def on_device(nope_query, rope_query, key_lift, value_lift, out_weight, latent_cache, lengths):
    cache = latent_cache[0].T
    in_hbm = (nope_query, rope_query, key_lift, value_lift, out_weight, cache)
    span = cache.shape[1]
    vmem = pl.BlockSpec(memory_space=pltpu.VMEM)
    hbm = pl.BlockSpec(memory_space=pltpu.HBM)
    return pl.pallas_call(
        kernel,
        out_shape=jax.ShapeDtypeStruct((Z, 2, COLS), F32),
        in_specs=[pl.BlockSpec(memory_space=pltpu.SMEM)] + [hbm] * 6,
        out_specs=vmem,
        scratch_shapes=[
            pltpu.VMEM(nope_query.shape, BF16),
            pltpu.VMEM(rope_query.shape, BF16),
            pltpu.VMEM(key_lift.shape, BF16),
            pltpu.VMEM(value_lift.shape, BF16),
            pltpu.VMEM(out_weight.shape, BF16),
            pltpu.VMEM((2, LAT + 128, span), BF16),
            pltpu.VMEM((2 * DV, 128 * G), BF16),
            pltpu.VMEM((N, 16, 128), BF16),
            pltpu.VMEM((N, 2, 128), F32),
            pltpu.VMEM((N, 16, 128), BF16),
            pltpu.VMEM((N, 16, 128), BF16),
            pltpu.VMEM((N, 1, 128), F32),
            pltpu.VMEM((N, 1, 128), F32),
            pltpu.VMEM((Z, 2, 2 * DV), F32),
            pltpu.VMEM((G, Y, 2, 128), F32),
            pltpu.VMEM((G * Y, 2, 128), F32),
            pltpu.SemaphoreType.DMA((6,)),
            pltpu.SemaphoreType.DMA((13,)),
            pltpu.SemaphoreType.DMA((13,)),
        ],
        compiler_params=pltpu.CompilerParams(
            collective_id=0, has_side_effects=True, vmem_limit_bytes=32 << 20
        ),
        cost_estimate=pl.CostEstimate(flops=600_000_000, bytes_accessed=2_500_000, transcendentals=300_000),
    )(lengths, *(pltpu.with_memory_space_constraint(a, pltpu.HBM) for a in in_hbm))


def solution(mesh):
    in_specs = (
        P("rows", None, "ctx", None),
        P("rows", None, "ctx", None),
        P("ctx", None, None),
        P("ctx", None, None),
        P("ctx", "rows"),
        P("rows", "ctx", None),
        P("rows"),
    )
    out_specs = P(None, None, ("rows", "ctx"))
    return jax.shard_map(
        on_device, mesh=mesh, in_specs=in_specs, out_specs=out_specs, check_vma=False
    )
```

```python
import functools

import jax
import jax.numpy as jnp
from jax import lax
from jax.experimental import pallas as pl
from jax.experimental.pallas import tpu as pltpu
from jax.sharding import PartitionSpec as P

DN = 128
DR = 64
LAT = 512
DV = 128
X, Y, Z = 4, 8, 8
G = 2 * X
COLS = 14
LOG2E = 1.4426950408889634
LOWEST = -1e30

MESH = pl.DeviceIdType.MESH
F32 = jnp.float32
BF16 = jnp.bfloat16

AWAY = [(dx, dc) for dx in range(X) for dc in range(2)]
SAME = [(dx, dy) for dx in range(X) for dy in range(Y)]
N = len(SAME)


def iota(shape, axis):
    return lax.broadcasted_iota(jnp.int32, shape, axis)


def dot(a, b):
    return jnp.dot(a, b, preferred_element_type=F32)


def hops(d, n):
    return min(d, n - d)


def farthest_first(n):
    return sorted(range(1, n), key=lambda d: -hops(d, n))


def one_where(condition):
    return jnp.where(condition, 1.0, 0.0).astype(BF16)


def split_three(value):
    high = value.astype(BF16)
    rest = value - high.astype(F32)
    middle = rest.astype(BF16)
    low = (rest - middle.astype(F32)).astype(BF16)
    return high, middle, low


def blocks_transposed(tile):
    row, block = iota((8, 128), 0), iota((8, 128), 1) >> 4
    for step in (1, 2, 4):
        above = pltpu.roll(pltpu.roll(tile, 8 - step, 0), 16 * step, 1)
        below = pltpu.roll(pltpu.roll(tile, step, 0), 128 - 16 * step, 1)
        stays = (row & step) == (block & step)
        tile = jnp.where(stays, tile, jnp.where((row & step) == 0, above, below))
    return tile


def kernel(
    lengths,
    nope_hbm,
    rope_hbm,
    key_lift_hbm,
    value_lift_hbm,
    weight_hbm,
    cache_hbm,
    out,
    nope,
    rope,
    key_lift,
    value_lift,
    weight,
    cache,
    placed,
    latents,
    rotaries,
    part_out,
    part_in,
    stat_out,
    stat_in,
    heads,
    sums_out,
    sums_in,
    local_sem,
    send_sem,
    recv_sem,
):
    row = lax.axis_index("rows")
    ctx = lax.axis_index("ctx")
    core = ctx & 1
    y = (ctx >> 1) & (Y - 1)
    x = ctx >> Y.bit_length()

    def in_plane(dx, dy, dc=0):
        to_x, to_y, to_core = (x + dx) & (X - 1), (y + dy) & (Y - 1), (core + dc) & 1
        return (row, (to_x * Y + to_y) * 2 + to_core)

    def along_z(d):
        return ((row + d) & (Z - 1), ctx)

    loads = [
        pltpu.make_async_copy(key_lift_hbm, key_lift, local_sem.at[0]),
        pltpu.make_async_copy(cache_hbm, cache.at[0, pl.ds(0, LAT + DR)], local_sem.at[1]),
        pltpu.make_async_copy(weight_hbm, weight, local_sem.at[2]),
        pltpu.make_async_copy(value_lift_hbm, value_lift, local_sem.at[3]),
        pltpu.make_async_copy(nope_hbm, nope, local_sem.at[4]),
        pltpu.make_async_copy(rope_hbm, rope, local_sem.at[5]),
    ]
    for at in (0, 4, 5):
        loads[at].start()

    barrier = pltpu.get_barrier_semaphore()
    far = sorted(range(1, N), key=lambda at: -hops(SAME[at][0], X) - hops(SAME[at][1], Y))
    partners = (
        [in_plane(*SAME[at]) for at in far]
        + [along_z(d) for d in farthest_first(Z)]
        + [in_plane(0, 0, 1)]
    )
    for partner in partners:
        pl.semaphore_signal(barrier, inc=1, device_id=partner, device_id_type=MESH)
    for at in (1, 2, 3):
        loads[at].start()

    def send(stage, source, target, device):
        pltpu.make_async_remote_copy(
            src_ref=source,
            dst_ref=target,
            send_sem=send_sem.at[stage],
            recv_sem=recv_sem.at[stage],
            device_id=device,
            device_id_type=MESH,
        ).start()

    def wait_all(sems, stage, buffer):
        slots = buffer.at[pl.ds(1, buffer.shape[0] - 1)]
        pltpu.make_async_copy(slots, slots, sems.at[stage]).wait()

    row16 = iota((16, 128), 0)
    even = (row16 & 1) == 0
    for at in (4, 5, 0):
        loads[at].wait()
    nope_rows = nope[0].astype(F32)
    rope_rows = rope[0].astype(F32)
    rotary = [jnp.concatenate([rope_rows[j, h : h + 1, :] for h in range(2)], axis=1) for j in range(2)]
    rotaries[0] = jnp.concatenate(rotary, axis=0).astype(BF16)
    latent = jnp.zeros((16, 128), F32)
    for h in range(2):
        left = jnp.where(
            even,
            jnp.broadcast_to(nope_rows[0, h : h + 1, :], (16, DN)),
            jnp.broadcast_to(nope_rows[1, h : h + 1, :], (16, DN)),
        ).astype(BF16)
        lifted = dot(left, key_lift[h])
        for c in range(4):
            latent = jnp.where(
                (row16 >> 1) == 2 * c + h, lifted[:, 128 * c : 128 * (c + 1)], latent
            )
    latents[0] = latent.astype(BF16)
    for part in range(2):
        cache[part, LAT + DR :, :] = jnp.zeros((128 - DR, cache.shape[2]), BF16)

    pl.semaphore_wait(barrier, len(partners))

    sibling_cache = cache.at[1, pl.ds(0, LAT + DR)]
    quarter = (LAT + DR) // 4
    for start in range(0, LAT + DR, quarter):
        rows = pl.ds(start, quarter)
        send(2, cache_hbm.at[rows], cache.at[1, rows], in_plane(0, 0, 1))

    for at in far:
        device = in_plane(*SAME[at])
        send(0, latents.at[0], latents.at[at], device)
        send(1, rotaries.at[0], rotaries.at[at], device)

    loads[2].wait()
    span = Y * 2 * COLS
    for ax in range(X):
        low = ax * span // 128 * 128
        high = min(-(-(ax + 1) * span // 128) * 128, X * span)
        n = iota((high - low, 256), 0) + low
        lane = iota((1, 256), 1)
        to_core, to_y, column = lane >> 7, (y + ((lane & 127) >> 4)) & (Y - 1), lane & 15
        source = ((ax * Y + to_y) * 2 + to_core) * COLS + column
        source = jnp.where(column < COLS, source, -1)
        choose = one_where(n == source)
        placed[:, 256 * ax : 256 * (ax + 1)] = dot(weight[:, low:high], choose).astype(BF16)

    r, k = iota((128, 128), 0), iota((128, 128), 1)
    spread = one_where(k == ((r >> 2) & 7) * 16 + (r >> 5) * 4 + (r & 3))
    gather = one_where(r == ((k >> 2) & 7) * 16 + (k >> 5) * 4 + (k & 3))
    turn = one_where(iota((4 * N, 2 * N), 1) == (iota((4 * N, 2 * N), 0) >> 2) * 2 + (iota((4 * N, 2 * N), 0) & 1))
    by_slot = one_where(iota((N, 4 * N), 0) == iota((N, 4 * N), 1) >> 2)

    loads[1].wait()
    span = cache.shape[2]
    block = span // 2
    count = 4 * N
    limit = lengths[0] - 1 + (iota((count, 1), 0) & 1)
    scale = LOG2E * (DN + DR) ** -0.5
    pltpu.make_async_copy(sibling_cache, sibling_cache, recv_sem.at[2]).wait()
    wait_all(recv_sem, 1, rotaries)
    wait_all(recv_sem, 0, latents)
    pieces = [dot(spread, latents[8 * at : 8 * at + 8].reshape(128, 128)).astype(BF16) for at in range(N // 8)]
    pieces = [
        jnp.concatenate([piece[32 * c : 32 * (c + 1)] for piece in pieces], axis=0) for c in range(4)
    ]
    turned = dot(turn, rotaries[...].reshape(2 * N, 128))
    second_head = (iota((count, 1), 0) & 2) > 0
    pieces.append(jnp.where(second_head, pltpu.roll(turned, DR, 1), turned).astype(BF16))
    query = jnp.concatenate(pieces, axis=1)
    tops, denominators, weighted = [], [], []
    for part in range(2):
        owner = ctx if part == 0 else ctx + 1 - 2 * core
        for start in range(0, span, block):
            visible = iota((1, block), 1) + (owner * span + start) < limit
            keys = cache[part, :, start : start + block]
            scores = jnp.where(visible, dot(query, keys) * scale, LOWEST)
            top = jnp.max(scores, axis=1, keepdims=True)
            expo = jnp.exp2(scores - top)
            tops.append(top)
            denominators.append(jnp.sum(expo, axis=1, keepdims=True))
            weighted.append(
                lax.dot_general(
                    expo.astype(BF16), keys[0:LAT], (((1,), (1,)), ((), ())), preferred_element_type=F32
                )
            )
    top = functools.reduce(jnp.maximum, tops)
    factors = [jnp.exp2(t - top) for t in tops]
    denominator = functools.reduce(jnp.add, [f * d for f, d in zip(factors, denominators)])
    total = functools.reduce(jnp.add, [f * w for f, w in zip(factors, weighted)])
    total = (total * (1.0 / denominator)).astype(BF16)
    for at in range(N // 8):
        rows = total[32 * at : 32 * at + 32]
        rows = jnp.concatenate([rows[:, 128 * c : 128 * (c + 1)] for c in range(4)], axis=0)
        part_out[8 * at : 8 * at + 8] = dot(gather, rows).astype(BF16).reshape(8, 16, 128)
    k, lane = iota((count, 128), 0), iota((count, 128), 1)
    stat = jnp.where((k & 3) == (lane & 3), top + jnp.log2(denominator), 0.0)
    stat_out[:, 0, :] = functools.reduce(jnp.add, [dot(by_slot, piece) for piece in split_three(stat)])

    for at in far:
        dx, dy = SAME[at]
        device = in_plane(X - dx, Y - dy)
        send(6, stat_out.at[at], stat_in.at[at], device)
        send(3, part_out.at[at], part_in.at[at], device)
    part_in[0] = part_out[0]
    stat_in[0] = stat_out[0]
    wait_all(send_sem, 0, latents)
    wait_all(send_sem, 1, rotaries)
    pltpu.make_async_copy(sibling_cache, sibling_cache, send_sem.at[2]).wait()
    loads[3].wait()
    wait_all(recv_sem, 6, stat_in)
    stat = stat_in[:, 0, :]
    factor = jnp.exp2(stat - jnp.max(stat, axis=0, keepdims=True))
    factor = (factor * (1.0 / jnp.sum(factor, axis=0, keepdims=True))).T[0:16]
    wait_all(recv_sem, 3, part_in)
    latent_out = functools.reduce(
        jnp.add, [factor[:, at : at + 1] * part_in[at].astype(F32) for at in range(N)]
    )
    wide = jnp.concatenate([jnp.where(row16 >> 2 == c, latent_out, 0.0) for c in range(4)], axis=1).astype(BF16)
    for h in range(2):
        lifted = dot(wide, value_lift[h])
        lifted = lifted + pltpu.roll(lifted, 8, 0)
        lifted = lifted + pltpu.roll(lifted, 4, 0)
        heads[0, :, DV * h : DV * (h + 1)] = lifted[2 * h : 2 * h + 2].astype(BF16).astype(F32)

    for d in farthest_first(Z):
        send(4, heads.at[0], heads.at[d], along_z(d))
    wait_all(send_sem, 3, part_in)
    wait_all(send_sem, 6, stat_in)
    wait_all(recv_sem, 4, heads)
    every = jnp.concatenate([heads[d] for d in range(Z)], axis=0).astype(BF16)
    product = dot(every, placed[...])
    for g in range(G):
        tiles = [product[8 * half : 8 * half + 8, 128 * g : 128 * (g + 1)] for half in range(2)]
        sums_out[g] = jnp.stack([blocks_transposed(tile) for tile in tiles], axis=1).astype(BF16)

    plane = [(g, d) for g in range(G) for d in range(Y)][1:]
    for g, d in sorted(plane, key=lambda at: -hops(AWAY[at[0]][0], X) - hops(at[1], Y)):
        dx, dc = AWAY[g]
        chunk = ((x + dx) & (X - 1)) * 2 + ((core + dc) & 1)
        send(5, sums_out.at[chunk, d], sums_in.at[g * Y + d], in_plane(dx, d, dc))
    wait_all(send_sem, 4, heads)
    wait_all(recv_sem, 5, sums_in)
    sums_in[0] = sums_out[x * 2 + core, 0]
    total = jnp.sum(sums_in[...].astype(F32), axis=0)
    for half in range(2):
        wide = jnp.broadcast_to(total[half : half + 1], (8, 128))
        wide = pltpu.roll(wide, 16, 1, stride=16, stride_axis=0)
        for at in range(8):
            sequence = (row - (4 * half + at // 2)) & (Z - 1)
            out[sequence, at % 2 : at % 2 + 1, :] = wide[7 - at : 8 - at, 0:COLS]
    wait_all(send_sem, 5, sums_in)


def on_device(nope_query, rope_query, key_lift, value_lift, out_weight, latent_cache, lengths):
    cache = latent_cache[0].T
    in_hbm = (nope_query, rope_query, key_lift, value_lift, out_weight, cache)
    span = cache.shape[1]
    vmem = pl.BlockSpec(memory_space=pltpu.VMEM)
    hbm = pl.BlockSpec(memory_space=pltpu.HBM)
    return pl.pallas_call(
        kernel,
        out_shape=jax.ShapeDtypeStruct((Z, 2, COLS), F32),
        in_specs=[pl.BlockSpec(memory_space=pltpu.SMEM)] + [hbm] * 6,
        out_specs=vmem,
        scratch_shapes=[
            pltpu.VMEM(nope_query.shape, BF16),
            pltpu.VMEM(rope_query.shape, BF16),
            pltpu.VMEM(key_lift.shape, BF16),
            pltpu.VMEM(value_lift.shape, BF16),
            pltpu.VMEM(out_weight.shape, BF16),
            pltpu.VMEM((2, LAT + 128, span), BF16),
            pltpu.VMEM((2 * DV, 128 * G), BF16),
            pltpu.VMEM((N, 16, 128), BF16),
            pltpu.VMEM((N, 2, 128), BF16),
            pltpu.VMEM((N, 16, 128), BF16),
            pltpu.VMEM((N, 16, 128), BF16),
            pltpu.VMEM((N, 1, 128), F32),
            pltpu.VMEM((N, 1, 128), F32),
            pltpu.VMEM((Z, 2, 2 * DV), F32),
            pltpu.VMEM((G, Y, 2, 128), BF16),
            pltpu.VMEM((G * Y, 2, 128), BF16),
            pltpu.SemaphoreType.DMA((6,)),
            pltpu.SemaphoreType.DMA((7,)),
            pltpu.SemaphoreType.DMA((7,)),
        ],
        compiler_params=pltpu.CompilerParams(
            collective_id=0, has_side_effects=True, vmem_limit_bytes=32 << 20
        ),
        cost_estimate=pl.CostEstimate(flops=600_000_000, bytes_accessed=2_500_000, transcendentals=300_000),
    )(lengths, *(pltpu.with_memory_space_constraint(a, pltpu.HBM) for a in in_hbm))


def solution(mesh):
    in_specs = (
        P("rows", None, "ctx", None),
        P("rows", None, "ctx", None),
        P("ctx", None, None),
        P("ctx", None, None),
        P("ctx", "rows"),
        P("rows", "ctx", None),
        P("rows"),
    )
    out_specs = P(None, None, ("rows", "ctx"))
    return jax.shard_map(
        on_device, mesh=mesh, in_specs=in_specs, out_specs=out_specs, check_vma=False
    )
```

```python
import functools

import jax
import jax.numpy as jnp
from jax import lax
from jax.experimental import pallas as pl
from jax.experimental.pallas import tpu as pltpu
from jax.sharding import PartitionSpec as P

DN = 128
DR = 64
LAT = 512
DV = 128
X, Y, Z = 4, 8, 8
G = 2 * X
COLS = 14
LOG2E = 1.4426950408889634
LOWEST = -1e30

MESH = pl.DeviceIdType.MESH
F32 = jnp.float32
BF16 = jnp.bfloat16

AWAY = [(dx, dc) for dx in range(X) for dc in range(2)]
SAME = [(dx, dy) for dx in range(X) for dy in range(Y)]
N = len(SAME)


def iota(shape, axis):
    return lax.broadcasted_iota(jnp.int32, shape, axis)


def dot(a, b):
    return jnp.dot(a, b, preferred_element_type=F32)


def hops(d, n):
    return min(d, n - d)


def farthest_first(n):
    return sorted(range(1, n), key=lambda d: -hops(d, n))


def one_where(condition):
    return jnp.where(condition, 1.0, 0.0).astype(BF16)


def split_three(value):
    high = value.astype(BF16)
    rest = value - high.astype(F32)
    middle = rest.astype(BF16)
    low = (rest - middle.astype(F32)).astype(BF16)
    return high, middle, low


def blocks_transposed(tile):
    row, block = iota((8, 128), 0), iota((8, 128), 1) >> 4
    for step in (1, 2, 4):
        above = pltpu.roll(pltpu.roll(tile, 8 - step, 0), 16 * step, 1)
        below = pltpu.roll(pltpu.roll(tile, step, 0), 128 - 16 * step, 1)
        stays = (row & step) == (block & step)
        tile = jnp.where(stays, tile, jnp.where((row & step) == 0, above, below))
    return tile


def kernel(
    lengths,
    nope_hbm,
    rope_hbm,
    key_lift_hbm,
    value_lift_hbm,
    weight_hbm,
    cache_hbm,
    out,
    nope,
    rope,
    key_lift,
    value_lift,
    weight,
    cache,
    placed,
    queries,
    part_out,
    part_in,
    stat_out,
    stat_in,
    heads,
    sums_out,
    sums_in,
    local_sem,
    send_sem,
    recv_sem,
):
    row = lax.axis_index("rows")
    ctx = lax.axis_index("ctx")
    core = ctx & 1
    y = (ctx >> 1) & (Y - 1)
    x = ctx >> Y.bit_length()

    def in_plane(dx, dy, dc=0):
        to_x, to_y, to_core = (x + dx) & (X - 1), (y + dy) & (Y - 1), (core + dc) & 1
        return (row, (to_x * Y + to_y) * 2 + to_core)

    def along_z(d):
        return ((row + d) & (Z - 1), ctx)

    loads = [
        pltpu.make_async_copy(key_lift_hbm, key_lift, local_sem.at[0]),
        pltpu.make_async_copy(cache_hbm, cache.at[0, pl.ds(0, LAT + DR)], local_sem.at[1]),
        pltpu.make_async_copy(weight_hbm, weight, local_sem.at[2]),
        pltpu.make_async_copy(value_lift_hbm, value_lift, local_sem.at[3]),
        pltpu.make_async_copy(nope_hbm, nope, local_sem.at[4]),
        pltpu.make_async_copy(rope_hbm, rope, local_sem.at[5]),
    ]
    for at in (0, 4, 5):
        loads[at].start()

    barrier = pltpu.get_barrier_semaphore()
    far = sorted(range(1, N), key=lambda at: -hops(SAME[at][0], X) - hops(SAME[at][1], Y))
    partners = (
        [in_plane(*SAME[at]) for at in far]
        + [along_z(d) for d in farthest_first(Z)]
        + [in_plane(0, 0, 1)]
    )
    for partner in partners:
        pl.semaphore_signal(barrier, inc=1, device_id=partner, device_id_type=MESH)
    for at in (1, 2, 3):
        loads[at].start()

    def send(stage, source, target, device):
        pltpu.make_async_remote_copy(
            src_ref=source,
            dst_ref=target,
            send_sem=send_sem.at[stage],
            recv_sem=recv_sem.at[stage],
            device_id=device,
            device_id_type=MESH,
        ).start()

    def wait_all(sems, stage, buffer):
        slots = buffer.at[pl.ds(1, buffer.shape[0] - 1)]
        pltpu.make_async_copy(slots, slots, sems.at[stage]).wait()

    row16 = iota((16, 128), 0)
    even = (row16 & 1) == 0
    for at in (4, 5, 0):
        loads[at].wait()
    nope_rows = nope[0].astype(F32)
    rope_rows = rope[0].astype(F32)
    rotary = [jnp.concatenate([rope_rows[j, h : h + 1, :] for h in range(2)], axis=1) for j in range(2)]
    queries[0, 16:18, :] = jnp.concatenate(rotary, axis=0).astype(BF16)
    latent = jnp.zeros((16, 128), F32)
    for h in range(2):
        left = jnp.where(
            even,
            jnp.broadcast_to(nope_rows[0, h : h + 1, :], (16, DN)),
            jnp.broadcast_to(nope_rows[1, h : h + 1, :], (16, DN)),
        ).astype(BF16)
        lifted = dot(left, key_lift[h])
        for c in range(4):
            latent = jnp.where(
                (row16 >> 1) == 2 * c + h, lifted[:, 128 * c : 128 * (c + 1)], latent
            )
    queries[0, 0:16, :] = latent.astype(BF16)
    for part in range(2):
        cache[part, LAT + DR :, :] = jnp.zeros((128 - DR, cache.shape[2]), BF16)

    pl.semaphore_wait(barrier, len(partners))

    sibling_cache = cache.at[1, pl.ds(0, LAT + DR)]
    quarter = (LAT + DR) // 4
    for start in range(0, LAT + DR, quarter):
        rows = pl.ds(start, quarter)
        send(2, cache_hbm.at[rows], cache.at[1, rows], in_plane(0, 0, 1))

    for at in far:
        send(0, queries.at[0], queries.at[at], in_plane(*SAME[at]))

    loads[2].wait()
    span = Y * 2 * COLS
    for ax in range(X):
        low = ax * span // 128 * 128
        high = min(-(-(ax + 1) * span // 128) * 128, X * span)
        n = iota((high - low, 256), 0) + low
        lane = iota((1, 256), 1)
        to_core, to_y, column = lane >> 7, (y + ((lane & 127) >> 4)) & (Y - 1), lane & 15
        source = ((ax * Y + to_y) * 2 + to_core) * COLS + column
        source = jnp.where(column < COLS, source, -1)
        choose = one_where(n == source)
        placed[:, 256 * ax : 256 * (ax + 1)] = dot(weight[:, low:high], choose).astype(BF16)

    r, k = iota((128, 128), 0), iota((128, 128), 1)
    spread = one_where(k == ((r >> 2) & 7) * 16 + (r >> 5) * 4 + (r & 3))
    gather = one_where(r == ((k >> 2) & 7) * 16 + (k >> 5) * 4 + (k & 3))
    turn = one_where(iota((4 * N, 2 * N), 1) == (iota((4 * N, 2 * N), 0) >> 2) * 2 + (iota((4 * N, 2 * N), 0) & 1))
    by_slot = one_where(iota((N, 4 * N), 0) == iota((N, 4 * N), 1) >> 2)

    loads[1].wait()
    span = cache.shape[2]
    block = span // 2
    count = 4 * N
    limit = lengths[0] - 1 + (iota((count, 1), 0) & 1)
    scale = LOG2E * (DN + DR) ** -0.5
    pltpu.make_async_copy(sibling_cache, sibling_cache, recv_sem.at[2]).wait()
    wait_all(recv_sem, 0, queries)
    pieces = [dot(spread, queries[8 * at : 8 * at + 8, 0:16].reshape(128, 128)).astype(BF16) for at in range(N // 8)]
    pieces = [
        jnp.concatenate([piece[32 * c : 32 * (c + 1)] for piece in pieces], axis=0) for c in range(4)
    ]
    turned = dot(turn, queries[:, 16:18].reshape(2 * N, 128))
    second_head = (iota((count, 1), 0) & 2) > 0
    pieces.append(jnp.where(second_head, pltpu.roll(turned, DR, 1), turned).astype(BF16))
    query = jnp.concatenate(pieces, axis=1)
    tops, denominators, weighted = [], [], []
    for part in range(2):
        owner = ctx if part == 0 else ctx + 1 - 2 * core
        for start in range(0, span, block):
            visible = iota((1, block), 1) + (owner * span + start) < limit
            keys = cache[part, :, start : start + block]
            scores = jnp.where(visible, dot(query, keys) * scale, LOWEST)
            top = jnp.max(scores, axis=1, keepdims=True)
            expo = jnp.exp2(scores - top)
            tops.append(top)
            denominators.append(jnp.sum(expo, axis=1, keepdims=True))
            weighted.append(
                lax.dot_general(
                    expo.astype(BF16), keys[0:LAT], (((1,), (1,)), ((), ())), preferred_element_type=F32
                )
            )
    top = functools.reduce(jnp.maximum, tops)
    factors = [jnp.exp2(t - top) for t in tops]
    denominator = functools.reduce(jnp.add, [f * d for f, d in zip(factors, denominators)])
    total = functools.reduce(jnp.add, [f * w for f, w in zip(factors, weighted)])
    total = (total * (1.0 / denominator)).astype(BF16)
    for at in range(N // 8):
        rows = total[32 * at : 32 * at + 32]
        rows = jnp.concatenate([rows[:, 128 * c : 128 * (c + 1)] for c in range(4)], axis=0)
        part_out[8 * at : 8 * at + 8] = dot(gather, rows).astype(BF16).reshape(8, 16, 128)
    k, lane = iota((count, 128), 0), iota((count, 128), 1)
    stat = jnp.where((k & 3) == (lane & 3), top + jnp.log2(denominator), 0.0)
    stat_out[:, 0, :] = functools.reduce(jnp.add, [dot(by_slot, piece) for piece in split_three(stat)])

    for at in far:
        dx, dy = SAME[at]
        device = in_plane(X - dx, Y - dy)
        send(6, stat_out.at[at], stat_in.at[at], device)
        send(3, part_out.at[at], part_in.at[at], device)
    part_in[0] = part_out[0]
    stat_in[0] = stat_out[0]
    wait_all(send_sem, 0, queries)
    pltpu.make_async_copy(sibling_cache, sibling_cache, send_sem.at[2]).wait()
    loads[3].wait()
    wait_all(recv_sem, 6, stat_in)
    stat = stat_in[:, 0, :]
    factor = jnp.exp2(stat - jnp.max(stat, axis=0, keepdims=True))
    factor = (factor * (1.0 / jnp.sum(factor, axis=0, keepdims=True))).T[0:16]
    wait_all(recv_sem, 3, part_in)
    latent_out = functools.reduce(
        jnp.add, [factor[:, at : at + 1] * part_in[at].astype(F32) for at in range(N)]
    )
    wide = jnp.concatenate([jnp.where(row16 >> 2 == c, latent_out, 0.0) for c in range(4)], axis=1).astype(BF16)
    for h in range(2):
        lifted = dot(wide, value_lift[h])
        lifted = lifted + pltpu.roll(lifted, 8, 0)
        lifted = lifted + pltpu.roll(lifted, 4, 0)
        heads[0, :, DV * h : DV * (h + 1)] = lifted[2 * h : 2 * h + 2].astype(BF16).astype(F32)

    for d in farthest_first(Z):
        send(4, heads.at[0], heads.at[d], along_z(d))
    wait_all(send_sem, 3, part_in)
    wait_all(send_sem, 6, stat_in)
    wait_all(recv_sem, 4, heads)
    every = jnp.concatenate([heads[d] for d in range(Z)], axis=0).astype(BF16)
    product = dot(every, placed[...])
    for g in range(G):
        tiles = [product[8 * half : 8 * half + 8, 128 * g : 128 * (g + 1)] for half in range(2)]
        sums_out[g] = jnp.stack([blocks_transposed(tile) for tile in tiles], axis=1).astype(BF16)

    plane = [(g, d) for g in range(G) for d in range(Y)][1:]
    for g, d in sorted(plane, key=lambda at: -hops(AWAY[at[0]][0], X) - hops(at[1], Y)):
        dx, dc = AWAY[g]
        chunk = ((x + dx) & (X - 1)) * 2 + ((core + dc) & 1)
        send(5, sums_out.at[chunk, d], sums_in.at[g * Y + d], in_plane(dx, d, dc))
    wait_all(send_sem, 4, heads)
    wait_all(recv_sem, 5, sums_in)
    sums_in[0] = sums_out[x * 2 + core, 0]
    total = jnp.sum(sums_in[...].astype(F32), axis=0)
    for half in range(2):
        wide = jnp.broadcast_to(total[half : half + 1], (8, 128))
        wide = pltpu.roll(wide, 16, 1, stride=16, stride_axis=0)
        for at in range(8):
            sequence = (row - (4 * half + at // 2)) & (Z - 1)
            out[sequence, at % 2 : at % 2 + 1, :] = wide[7 - at : 8 - at, 0:COLS]
    wait_all(send_sem, 5, sums_in)


def on_device(nope_query, rope_query, key_lift, value_lift, out_weight, latent_cache, lengths):
    cache = latent_cache[0].T
    in_hbm = (nope_query, rope_query, key_lift, value_lift, out_weight, cache)
    span = cache.shape[1]
    vmem = pl.BlockSpec(memory_space=pltpu.VMEM)
    hbm = pl.BlockSpec(memory_space=pltpu.HBM)
    return pl.pallas_call(
        kernel,
        out_shape=jax.ShapeDtypeStruct((Z, 2, COLS), F32),
        in_specs=[pl.BlockSpec(memory_space=pltpu.SMEM)] + [hbm] * 6,
        out_specs=vmem,
        scratch_shapes=[
            pltpu.VMEM(nope_query.shape, BF16),
            pltpu.VMEM(rope_query.shape, BF16),
            pltpu.VMEM(key_lift.shape, BF16),
            pltpu.VMEM(value_lift.shape, BF16),
            pltpu.VMEM(out_weight.shape, BF16),
            pltpu.VMEM((2, LAT + 128, span), BF16),
            pltpu.VMEM((2 * DV, 128 * G), BF16),
            pltpu.VMEM((N, 18, 128), BF16),
            pltpu.VMEM((N, 16, 128), BF16),
            pltpu.VMEM((N, 16, 128), BF16),
            pltpu.VMEM((N, 1, 128), F32),
            pltpu.VMEM((N, 1, 128), F32),
            pltpu.VMEM((Z, 2, 2 * DV), F32),
            pltpu.VMEM((G, Y, 2, 128), BF16),
            pltpu.VMEM((G * Y, 2, 128), BF16),
            pltpu.SemaphoreType.DMA((6,)),
            pltpu.SemaphoreType.DMA((7,)),
            pltpu.SemaphoreType.DMA((7,)),
        ],
        compiler_params=pltpu.CompilerParams(
            collective_id=0, has_side_effects=True, vmem_limit_bytes=32 << 20
        ),
        cost_estimate=pl.CostEstimate(flops=600_000_000, bytes_accessed=2_500_000, transcendentals=300_000),
    )(lengths, *(pltpu.with_memory_space_constraint(a, pltpu.HBM) for a in in_hbm))


def solution(mesh):
    in_specs = (
        P("rows", None, "ctx", None),
        P("rows", None, "ctx", None),
        P("ctx", None, None),
        P("ctx", None, None),
        P("ctx", "rows"),
        P("rows", "ctx", None),
        P("rows"),
    )
    out_specs = P(None, None, ("rows", "ctx"))
    return jax.shard_map(
        on_device, mesh=mesh, in_specs=in_specs, out_specs=out_specs, check_vma=False
    )
```

```python
import functools

import jax
import jax.numpy as jnp
from jax import lax
from jax.experimental import pallas as pl
from jax.experimental.pallas import tpu as pltpu
from jax.sharding import PartitionSpec as P

DN = 128
DR = 64
LAT = 512
DV = 128
X, Y, Z = 4, 8, 8
G = 2 * X
COLS = 14
LOG2E = 1.4426950408889634
LOWEST = -1e30

MESH = pl.DeviceIdType.MESH
F32 = jnp.float32
BF16 = jnp.bfloat16

AWAY = [(dx, dc) for dx in range(X) for dc in range(2)]
SAME = [(dx, dy) for dx in range(X) for dy in range(Y)]
N = len(SAME)


def iota(shape, axis):
    return lax.broadcasted_iota(jnp.int32, shape, axis)


def dot(a, b):
    return jnp.dot(a, b, preferred_element_type=F32)


def hops(d, n):
    return min(d, n - d)


def farthest_first(n):
    return sorted(range(1, n), key=lambda d: -hops(d, n))


def one_where(condition):
    return jnp.where(condition, 1.0, 0.0).astype(BF16)


def split_three(value):
    high = value.astype(BF16)
    rest = value - high.astype(F32)
    middle = rest.astype(BF16)
    low = (rest - middle.astype(F32)).astype(BF16)
    return high, middle, low


def blocks_transposed(tile):
    row, block = iota((8, 128), 0), iota((8, 128), 1) >> 4
    for step in (1, 2, 4):
        above = pltpu.roll(pltpu.roll(tile, 8 - step, 0), 16 * step, 1)
        below = pltpu.roll(pltpu.roll(tile, step, 0), 128 - 16 * step, 1)
        stays = (row & step) == (block & step)
        tile = jnp.where(stays, tile, jnp.where((row & step) == 0, above, below))
    return tile


def kernel(
    lengths,
    nope_hbm,
    rope_hbm,
    key_lift_hbm,
    value_lift_hbm,
    weight_hbm,
    cache_hbm,
    out,
    nope,
    rope,
    key_lift,
    value_lift,
    weight,
    cache,
    placed,
    latents,
    rotaries,
    part_out,
    part_in,
    stat_out,
    stat_in,
    heads,
    sums_out,
    sums_in,
    local_sem,
    send_sem,
    recv_sem,
):
    row = lax.axis_index("rows")
    ctx = lax.axis_index("ctx")
    core = ctx & 1
    y = (ctx >> 1) & (Y - 1)
    x = ctx >> Y.bit_length()

    def in_plane(dx, dy, dc=0):
        to_x, to_y, to_core = (x + dx) & (X - 1), (y + dy) & (Y - 1), (core + dc) & 1
        return (row, (to_x * Y + to_y) * 2 + to_core)

    def along_z(d):
        return ((row + d) & (Z - 1), ctx)

    loads = [
        pltpu.make_async_copy(key_lift_hbm, key_lift, local_sem.at[0]),
        pltpu.make_async_copy(cache_hbm, cache.at[0, pl.ds(0, LAT + DR)], local_sem.at[1]),
        pltpu.make_async_copy(weight_hbm, weight, local_sem.at[2]),
        pltpu.make_async_copy(value_lift_hbm, value_lift, local_sem.at[3]),
        pltpu.make_async_copy(nope_hbm, nope, local_sem.at[4]),
        pltpu.make_async_copy(rope_hbm, rope, local_sem.at[5]),
    ]
    for at in (0, 4, 5):
        loads[at].start()

    barrier = pltpu.get_barrier_semaphore()
    far = sorted(range(1, N), key=lambda at: -hops(SAME[at][0], X) - hops(SAME[at][1], Y))
    partners = (
        [in_plane(*SAME[at]) for at in far]
        + [along_z(d) for d in farthest_first(Z)]
        + [in_plane(0, 0, 1)]
    )
    for partner in partners:
        pl.semaphore_signal(barrier, inc=1, device_id=partner, device_id_type=MESH)
    for at in (1, 2, 3):
        loads[at].start()

    def send(stage, source, target, device):
        pltpu.make_async_remote_copy(
            src_ref=source,
            dst_ref=target,
            send_sem=send_sem.at[stage],
            recv_sem=recv_sem.at[stage],
            device_id=device,
            device_id_type=MESH,
        ).start()

    def wait_all(sems, stage, buffer):
        slots = buffer.at[pl.ds(1, buffer.shape[0] - 1)]
        pltpu.make_async_copy(slots, slots, sems.at[stage]).wait()

    row16 = iota((16, 128), 0)
    even = (row16 & 1) == 0
    for at in (4, 5, 0):
        loads[at].wait()
    nope_rows = nope[0].astype(F32)
    rope_rows = rope[0].astype(F32)
    rotary = [jnp.concatenate([rope_rows[j, h : h + 1, :] for h in range(2)], axis=1) for j in range(2)]
    rotaries[0] = jnp.concatenate(rotary, axis=0).astype(BF16)
    latent = jnp.zeros((16, 128), F32)
    for h in range(2):
        left = jnp.where(
            even,
            jnp.broadcast_to(nope_rows[0, h : h + 1, :], (16, DN)),
            jnp.broadcast_to(nope_rows[1, h : h + 1, :], (16, DN)),
        ).astype(BF16)
        lifted = dot(left, key_lift[h])
        for c in range(4):
            latent = jnp.where(
                (row16 >> 1) == 2 * c + h, lifted[:, 128 * c : 128 * (c + 1)], latent
            )
    latents[0] = latent.astype(BF16)
    for part in range(2):
        cache[part, LAT + DR :, :] = jnp.zeros((128 - DR, cache.shape[2]), BF16)

    pl.semaphore_wait(barrier, len(partners))

    sibling_cache = cache.at[1, pl.ds(0, LAT + DR)]
    quarter = (LAT + DR) // 4
    for start in range(0, LAT + DR, quarter):
        rows = pl.ds(start, quarter)
        send(2, cache_hbm.at[rows], cache.at[1, rows], in_plane(0, 0, 1))

    for at in far:
        device = in_plane(*SAME[at])
        send(0, latents.at[0], latents.at[at], device)
        send(1, rotaries.at[0], rotaries.at[at], device)

    loads[2].wait()
    span = Y * 2 * COLS
    for ax in range(X):
        low = ax * span // 128 * 128
        high = min(-(-(ax + 1) * span // 128) * 128, X * span)
        n = iota((high - low, 256), 0) + low
        lane = iota((1, 256), 1)
        to_core, to_y, column = lane >> 7, (y + ((lane & 127) >> 4)) & (Y - 1), lane & 15
        source = ((ax * Y + to_y) * 2 + to_core) * COLS + column
        source = jnp.where(column < COLS, source, -1)
        choose = one_where(n == source)
        placed[:, 256 * ax : 256 * (ax + 1)] = dot(weight[:, low:high], choose).astype(BF16)

    r, k = iota((128, 128), 0), iota((128, 128), 1)
    spread = one_where(k == ((r >> 2) & 7) * 16 + (r >> 5) * 4 + (r & 3))
    gather = one_where(r == ((k >> 2) & 7) * 16 + (k >> 5) * 4 + (k & 3))
    turn = one_where(iota((4 * N, 2 * N), 1) == (iota((4 * N, 2 * N), 0) >> 2) * 2 + (iota((4 * N, 2 * N), 0) & 1))
    by_slot = one_where(iota((N, 4 * N), 0) == iota((N, 4 * N), 1) >> 2)

    loads[1].wait()
    span = cache.shape[2]
    block = span // 2
    count = 4 * N
    limit = lengths[0] - 1 + (iota((count, 1), 0) & 1)
    scale = LOG2E * (DN + DR) ** -0.5
    pltpu.make_async_copy(sibling_cache, sibling_cache, recv_sem.at[2]).wait()
    wait_all(recv_sem, 1, rotaries)
    wait_all(recv_sem, 0, latents)
    pieces = [dot(spread, latents[8 * at : 8 * at + 8].reshape(128, 128)).astype(BF16) for at in range(N // 8)]
    pieces = [
        jnp.concatenate([piece[32 * c : 32 * (c + 1)] for piece in pieces], axis=0) for c in range(4)
    ]
    turned = dot(turn, rotaries[...].reshape(2 * N, 128))
    second_head = (iota((count, 1), 0) & 2) > 0
    pieces.append(jnp.where(second_head, pltpu.roll(turned, DR, 1), turned).astype(BF16))
    query = jnp.concatenate(pieces, axis=1)
    tops, denominators, weighted = [], [], []
    for part in range(2):
        owner = ctx if part == 0 else ctx + 1 - 2 * core
        for start in range(0, span, block):
            visible = iota((1, block), 1) + (owner * span + start) < limit
            keys = cache[part, :, start : start + block]
            scores = jnp.where(visible, dot(query, keys) * scale, LOWEST)
            top = jnp.max(scores, axis=1, keepdims=True)
            expo = jnp.exp2(scores - top)
            tops.append(top)
            denominators.append(jnp.sum(expo, axis=1, keepdims=True))
            weighted.append(
                lax.dot_general(
                    expo.astype(BF16), keys[0:LAT], (((1,), (1,)), ((), ())), preferred_element_type=F32
                )
            )
    top = functools.reduce(jnp.maximum, tops)
    factors = [jnp.exp2(t - top) for t in tops]
    denominator = functools.reduce(jnp.add, [f * d for f, d in zip(factors, denominators)])
    total = functools.reduce(jnp.add, [f * w for f, w in zip(factors, weighted)])
    total = (total * (1.0 / denominator)).astype(BF16)
    for at in range(N // 8):
        rows = total[32 * at : 32 * at + 32]
        rows = jnp.concatenate([rows[:, 128 * c : 128 * (c + 1)] for c in range(4)], axis=0)
        part_out[8 * at : 8 * at + 8] = dot(gather, rows).astype(BF16).reshape(8, 16, 128)
    k, lane = iota((count, 128), 0), iota((count, 128), 1)
    stat = jnp.where((k & 3) == (lane & 3), top + jnp.log2(denominator), 0.0)
    stat_out[:, 0, :] = functools.reduce(jnp.add, [dot(by_slot, piece) for piece in split_three(stat)])

    for at in far:
        dx, dy = SAME[at]
        device = in_plane(X - dx, Y - dy)
        send(6, stat_out.at[at], stat_in.at[at], device)
        send(3, part_out.at[at], part_in.at[at], device)
    part_in[0] = part_out[0]
    stat_in[0] = stat_out[0]
    wait_all(send_sem, 0, latents)
    wait_all(send_sem, 1, rotaries)
    pltpu.make_async_copy(sibling_cache, sibling_cache, send_sem.at[2]).wait()
    loads[3].wait()
    wait_all(recv_sem, 6, stat_in)
    stat = stat_in[:, 0, :]
    factor = jnp.exp2(stat - jnp.max(stat, axis=0, keepdims=True))
    factor = (factor * (1.0 / jnp.sum(factor, axis=0, keepdims=True))).T[0:16]
    wait_all(recv_sem, 3, part_in)
    latent_out = functools.reduce(
        jnp.add, [factor[:, at : at + 1] * part_in[at].astype(F32) for at in range(N)]
    )
    wide = jnp.concatenate([jnp.where(row16 >> 2 == c, latent_out, 0.0) for c in range(4)], axis=1).astype(BF16)
    for h in range(2):
        lifted = dot(wide, value_lift[h])
        lifted = lifted + pltpu.roll(lifted, 8, 0)
        lifted = lifted + pltpu.roll(lifted, 4, 0)
        heads[0, :, DV * h : DV * (h + 1)] = lifted[2 * h : 2 * h + 2].astype(BF16)

    for d in farthest_first(Z):
        send(4, heads.at[0], heads.at[d], along_z(d))
    wait_all(send_sem, 3, part_in)
    wait_all(send_sem, 6, stat_in)
    wait_all(recv_sem, 4, heads)
    every = jnp.concatenate([heads[d].astype(F32) for d in range(Z)], axis=0).astype(BF16)
    product = dot(every, placed[...])
    for g in range(G):
        tiles = [product[8 * half : 8 * half + 8, 128 * g : 128 * (g + 1)] for half in range(2)]
        sums_out[g] = jnp.stack([blocks_transposed(tile) for tile in tiles], axis=1).astype(BF16)

    plane = [(g, d) for g in range(G) for d in range(Y)][1:]
    for g, d in sorted(plane, key=lambda at: -hops(AWAY[at[0]][0], X) - hops(at[1], Y)):
        dx, dc = AWAY[g]
        chunk = ((x + dx) & (X - 1)) * 2 + ((core + dc) & 1)
        send(5, sums_out.at[chunk, d], sums_in.at[g * Y + d], in_plane(dx, d, dc))
    wait_all(send_sem, 4, heads)
    wait_all(recv_sem, 5, sums_in)
    sums_in[0] = sums_out[x * 2 + core, 0]
    total = jnp.sum(sums_in[...].astype(F32), axis=0)
    for half in range(2):
        wide = jnp.broadcast_to(total[half : half + 1], (8, 128))
        wide = pltpu.roll(wide, 16, 1, stride=16, stride_axis=0)
        for at in range(8):
            sequence = (row - (4 * half + at // 2)) & (Z - 1)
            out[sequence, at % 2 : at % 2 + 1, :] = wide[7 - at : 8 - at, 0:COLS]
    wait_all(send_sem, 5, sums_in)


def on_device(nope_query, rope_query, key_lift, value_lift, out_weight, latent_cache, lengths):
    cache = latent_cache[0].T
    in_hbm = (nope_query, rope_query, key_lift, value_lift, out_weight, cache)
    span = cache.shape[1]
    vmem = pl.BlockSpec(memory_space=pltpu.VMEM)
    hbm = pl.BlockSpec(memory_space=pltpu.HBM)
    return pl.pallas_call(
        kernel,
        out_shape=jax.ShapeDtypeStruct((Z, 2, COLS), F32),
        in_specs=[pl.BlockSpec(memory_space=pltpu.SMEM)] + [hbm] * 6,
        out_specs=vmem,
        scratch_shapes=[
            pltpu.VMEM(nope_query.shape, BF16),
            pltpu.VMEM(rope_query.shape, BF16),
            pltpu.VMEM(key_lift.shape, BF16),
            pltpu.VMEM(value_lift.shape, BF16),
            pltpu.VMEM(out_weight.shape, BF16),
            pltpu.VMEM((2, LAT + 128, span), BF16),
            pltpu.VMEM((2 * DV, 128 * G), BF16),
            pltpu.VMEM((N, 16, 128), BF16),
            pltpu.VMEM((N, 2, 128), BF16),
            pltpu.VMEM((N, 16, 128), BF16),
            pltpu.VMEM((N, 16, 128), BF16),
            pltpu.VMEM((N, 1, 128), F32),
            pltpu.VMEM((N, 1, 128), F32),
            pltpu.VMEM((Z, 2, 2 * DV), BF16),
            pltpu.VMEM((G, Y, 2, 128), BF16),
            pltpu.VMEM((G * Y, 2, 128), BF16),
            pltpu.SemaphoreType.DMA((6,)),
            pltpu.SemaphoreType.DMA((7,)),
            pltpu.SemaphoreType.DMA((7,)),
        ],
        compiler_params=pltpu.CompilerParams(
            collective_id=0, has_side_effects=True, vmem_limit_bytes=32 << 20
        ),
        cost_estimate=pl.CostEstimate(flops=600_000_000, bytes_accessed=2_500_000, transcendentals=300_000),
    )(lengths, *(pltpu.with_memory_space_constraint(a, pltpu.HBM) for a in in_hbm))


def solution(mesh):
    in_specs = (
        P("rows", None, "ctx", None),
        P("rows", None, "ctx", None),
        P("ctx", None, None),
        P("ctx", None, None),
        P("ctx", "rows"),
        P("rows", "ctx", None),
        P("rows"),
    )
    out_specs = P(None, None, ("rows", "ctx"))
    return jax.shard_map(
        on_device, mesh=mesh, in_specs=in_specs, out_specs=out_specs, check_vma=False
    )
```
